256 devices in a mesh: tm: 16 (over y_lo, z), rows: 16 (over x, y_hi, core).
Axes of the slice: x: 4, y: 4 (y_hi: 2, y_lo: 2; y = y_hi * 2 + y_lo), z: 8, core: 2. Of those that a mesh axis runs over, the one named last changes fastest.
Arguments:
- queries: bfloat16 [16, 128, 16, 3072], P('tm', 'rows'), may hold values from -6 to 6
- key_states: bfloat16 [16, 128, 16, 3072], P('tm', 'rows'), may hold values from -6 to 6
- value_states: bfloat16 [16, 128, 16, 3072], P('tm', 'rows'), may hold values from -12 to 12
- out_grad: bfloat16 [16, 128, 16, 3072], P('tm', 'rows'), may hold values from -6 to 6
Outputs:
- temporal_out: bfloat16 [16, 128, 16, 3072], P('tm', 'rows')
- query_grad: bfloat16 [16, 128, 16, 3072], P('tm', 'rows')
- key_grad: bfloat16 [16, 128, 16, 3072], P('tm', 'rows')
- value_grad: bfloat16 [16, 128, 16, 3072], P('tm', 'rows')
The draws below stay inside these ranges and needn't reach their ends.
All inputs are finite; a program needn't handle non-finite values.
Results may differ from the reference program's by a relative error of at most 0.02.
Values may be sent and summed in bfloat16 or wider, within the bound.
No kernel may reach another device: no remote copies, remote signals or barrier semaphores. Data moves between devices by JAX's collectives and lax.ppermute only.
A program may use at most 128 MiB of HBM per device.

```python
import jax
import jax.numpy as jnp
from jax import lax

HEADS = 24
HEAD_DIM = 128
COLS = 16
RADIUS = 3
WIDTH = 3072
ROWS = 128
FRAMES = 16


def draw_queries(key, part):
    full_shape = (FRAMES, ROWS, COLS, HEADS * HEAD_DIM)
    drawn = 1.4 * jax.random.normal(jax.random.fold_in(key, 1), full_shape, jnp.float32)
    return jnp.clip(drawn, -6.0, 6.0).astype(jnp.bfloat16)


def draw_key_states(key, part):
    full_shape = (FRAMES, ROWS, COLS, HEADS * HEAD_DIM)
    drawn = 1.4 * jax.random.normal(jax.random.fold_in(key, 3), full_shape, jnp.float32)
    return jnp.clip(drawn, -6.0, 6.0).astype(jnp.bfloat16)


def block_levels(key, shape, shards, smallest, top_value):
    def one(axis_at, parts):
        heights = jax.random.uniform(jax.random.fold_in(jax.random.fold_in(key, 6), axis_at), (parts,), jnp.float32, smallest / len(shards), top_value / len(shards))
        return jnp.repeat(jnp.exp(heights), shape[axis_at] // parts).reshape((-1,) + (1,) * (len(shape) - axis_at - 1))

    factor_of = one(*shards[0])
    for cut in shards[1:]:
        factor_of = factor_of * one(*cut)
    return factor_of


def noise(own_key, shape, width, most, shards=(), kind=jnp.bfloat16):
    loudness = block_levels(own_key, shape, shards, -0.22, 0.18) if shards else 1.0
    array = jax.random.normal(own_key, shape, jnp.float32) * width * loudness
    return jnp.minimum(jnp.maximum(array, -most), most).astype(kind)


def setup_inputs(seed: int = 0) -> dict:
    arg_keys = jax.random.split(jax.random.key(seed), 5)
    queries = draw_queries(jax.random.fold_in(arg_keys[4], 71), 0)
    key_states = draw_key_states(jax.random.fold_in(arg_keys[4], 71), 0)
    value_states = noise(arg_keys[2], (FRAMES, ROWS, COLS, WIDTH), 2.0, 12.0, ((0, 16), (1, 16)))
    out_grad = noise(arg_keys[3], (FRAMES, ROWS, COLS, WIDTH), 1.0, 6.0, ((0, 16), (1, 16)))
    return {"queries": queries, "key_states": key_states, "value_states": value_states, "out_grad": out_grad}


NEG_FILL = -1.0e30


def window_offsets():
    return [(row_step, col_step) for row_step in range(-RADIUS, RADIUS + 1) for col_step in range(-RADIUS, RADIUS + 1)]


def shifted(tensor, row_step, col_step):
    height, breadth = tensor.shape[0], tensor.shape[1]
    widths = [(RADIUS, RADIUS), (RADIUS, RADIUS)] + [(0, 0)] * (tensor.ndim - 2)
    padded = jnp.pad(tensor, widths)
    return padded[RADIUS + row_step:RADIUS + row_step + height, RADIUS + col_step:RADIUS + col_step + breadth]


def inside_grid(height, breadth, row_step, col_step):
    row_index = jnp.arange(height) + row_step
    col_index = jnp.arange(breadth) + col_step
    row_fine = (row_index >= 0) & (row_index < height)
    col_fine = (col_index >= 0) & (col_index < breadth)
    return row_fine[:, None, None] & col_fine[None, :, None]


def split_heads(tensor):
    return tensor.astype(jnp.float32).reshape(tensor.shape[0], tensor.shape[1], HEADS, HEAD_DIM)


def round_keep(tensor):
    return lax.optimization_barrier(tensor.astype(jnp.bfloat16)).astype(jnp.float32)


def spatial_forward(frame_data):
    query_frame, key_frame, value_frame = frame_data
    height, breadth = query_frame.shape[0], query_frame.shape[1]
    scaling = HEAD_DIM ** -0.5
    query_heads = split_heads(query_frame)
    score_list = []
    for row_step, col_step in window_offsets():
        key_heads = split_heads(shifted(key_frame, row_step, col_step))
        inside = inside_grid(height, breadth, row_step, col_step)
        score_list.append(jnp.where(inside, jnp.sum(query_heads * key_heads, -1) * scaling, NEG_FILL))
    scores = jnp.stack(score_list)
    peak_score = jnp.max(scores, 0)
    log_total = peak_score + jnp.log(jnp.sum(jnp.exp(scores - peak_score), 0))
    weights = round_keep(jnp.exp(scores - log_total))
    summed = jnp.zeros(query_heads.shape, jnp.float32)
    for position, (row_step, col_step) in enumerate(window_offsets()):
        summed = summed + weights[position][..., None] * split_heads(shifted(value_frame, row_step, col_step))
    return summed.reshape(height, breadth, HEADS * HEAD_DIM).astype(jnp.bfloat16), log_total


def temporal_row(row_data):
    query_row, key_row, spatial_row, grad_row = row_data
    frames_all, breadth = query_row.shape[0], query_row.shape[1]
    scaling = HEAD_DIM ** -0.5
    query_heads = split_heads(query_row)
    key_heads = split_heads(key_row)
    spatial_heads = split_heads(spatial_row)
    grad_heads = split_heads(grad_row)
    scores = jnp.einsum("fchd,gchd->chfg", query_heads, key_heads) * scaling
    peak_score = jnp.max(scores, -1, keepdims=True)
    log_total = peak_score + jnp.log(jnp.sum(jnp.exp(scores - peak_score), -1, keepdims=True))
    probs_time = jnp.exp(scores - log_total)
    weights = round_keep(probs_time)
    temporal_out = jnp.einsum("chfg,gchd->fchd", weights, spatial_heads).astype(jnp.bfloat16)
    grad_dot = jnp.sum(grad_heads * lax.optimization_barrier(temporal_out).astype(jnp.float32), -1)
    prob_grad = jnp.einsum("fchd,gchd->chfg", grad_heads, spatial_heads)
    score_grad = round_keep(probs_time * (prob_grad - jnp.transpose(grad_dot, (1, 2, 0))[..., None]))
    spatial_grad = jnp.einsum("chfg,fchd->gchd", weights, grad_heads).astype(jnp.bfloat16)
    query_part = (jnp.einsum("chfg,gchd->fchd", score_grad, key_heads) * scaling).astype(jnp.bfloat16)
    key_part = (jnp.einsum("chfg,fchd->gchd", score_grad, query_heads) * scaling).astype(jnp.bfloat16)
    shape_back = (frames_all, breadth, HEADS * HEAD_DIM)
    return (temporal_out.reshape(shape_back), spatial_grad.reshape(shape_back), query_part.reshape(shape_back), key_part.reshape(shape_back))


def spatial_backward(frame_data):
    query_frame, key_frame, value_frame, spatial_frame, log_total, grad_frame = frame_data
    height, breadth = query_frame.shape[0], query_frame.shape[1]
    scaling = HEAD_DIM ** -0.5
    query_heads = split_heads(query_frame)
    grad_heads = split_heads(grad_frame)
    grad_dot = jnp.sum(grad_heads * split_heads(spatial_frame), -1)
    query_sum = jnp.zeros(query_heads.shape, jnp.float32)
    key_sum = jnp.zeros(query_heads.shape, jnp.float32)
    value_sum = jnp.zeros(query_heads.shape, jnp.float32)
    for row_step, col_step in window_offsets():
        key_heads = split_heads(shifted(key_frame, row_step, col_step))
        value_heads = split_heads(shifted(value_frame, row_step, col_step))
        inside = inside_grid(height, breadth, row_step, col_step)
        scores = jnp.where(inside, jnp.sum(query_heads * key_heads, -1) * scaling, NEG_FILL)
        probs_space = jnp.exp(scores - log_total)
        weights = round_keep(probs_space)
        prob_grad = jnp.sum(grad_heads * value_heads, -1)
        score_grad = round_keep(probs_space * (prob_grad - grad_dot))
        query_sum = query_sum + score_grad[..., None] * key_heads
        key_sum = key_sum + shifted(score_grad[..., None] * query_heads, -row_step, -col_step)
        value_sum = value_sum + shifted(weights[..., None] * grad_heads, -row_step, -col_step)
    shape_back = (height, breadth, HEADS * HEAD_DIM)
    return ((query_sum * scaling).reshape(shape_back), (key_sum * scaling).reshape(shape_back), value_sum.reshape(shape_back))


def reference(queries, key_states, value_states, out_grad):
    spatial_out, log_totals = lax.map(spatial_forward, (queries, key_states, value_states))
    row_inputs = tuple(jnp.swapaxes(tensor, 0, 1) for tensor in (queries, key_states, spatial_out, out_grad))
    temporal_rows = lax.map(temporal_row, row_inputs)
    temporal_out, spatial_grad, query_part, key_part = (jnp.swapaxes(tensor, 0, 1) for tensor in temporal_rows)
    query_spatial, key_spatial, value_spatial = lax.map(spatial_backward, (queries, key_states, value_states, spatial_out, log_totals, spatial_grad))
    query_grad = (query_spatial + query_part.astype(jnp.float32)).astype(jnp.bfloat16)
    key_grad = (key_spatial + key_part.astype(jnp.float32)).astype(jnp.bfloat16)
    value_grad = value_spatial.astype(jnp.bfloat16)
    return (temporal_out, query_grad, key_grad, value_grad)
```

```python
import functools

import jax
import jax.numpy as jnp
from jax import lax
from jax.experimental import pallas as pl
from jax.experimental.pallas import tpu as pltpu
from jax.sharding import PartitionSpec as P

HEADS = 24
HEAD_DIM = 128
RADIUS = 3
SCALING = HEAD_DIM ** (-0.5)
NEG_FILL = -1e30
BF16 = jnp.bfloat16
F32 = jnp.float32

FWD_HEADS = 4
SCORE_HEADS = 4
TIME_HEADS = 4
BWD_HEADS = 4
RIM_HEADS = 8
LAST_HEADS = 6

NT = (((1,), (1,)), ((), ()))
NN = (((1,), (0,)), ((), ()))
TN = (((0,), (0,)), ((), ()))


def dot(left, right, dims):
    return lax.dot_general(left, right, dims, preferred_element_type=F32)


def lanes(head):
    return slice(head * HEAD_DIM, (head + 1) * HEAD_DIM)


def flat_rows(chunks):
    wide = chunks.astype(F32)
    return wide.reshape(wide.shape[0] * wide.shape[1], wide.shape[2])


def chunked(matrix, chunks):
    return matrix.reshape(chunks, matrix.shape[0] // chunks, matrix.shape[1])


def softmax_columns(scores):
    peak = jnp.max(scores, 0, keepdims=True)
    grown = jnp.exp((scores - peak) * SCALING)
    return grown * (1.0 / jnp.sum(grown, 0, keepdims=True))


def call(kernel, grid, in_specs, out_specs, out_shape, **more):
    return pl.pallas_call(
        kernel,
        grid=(grid,),
        in_specs=in_specs,
        out_specs=out_specs,
        out_shape=out_shape,
        compiler_params=pltpu.CompilerParams(vmem_limit_bytes=48 * 1024 * 1024),
        **more,
    )


def window_mask(first_row, total_rows, breadth, keys, queries):
    key = lax.broadcasted_iota(jnp.int32, (keys, queries), 0)
    query = lax.broadcasted_iota(jnp.int32, (keys, queries), 1)
    row_step = key // breadth - RADIUS - query // breadth
    col_step = key % breadth - query % breadth
    key_row = first_row - RADIUS + key // breadth
    return (
        (jnp.abs(row_step) <= RADIUS)
        & (jnp.abs(col_step) <= RADIUS)
        & (key_row >= 0)
        & (key_row < total_rows)
    )


def window_of(own_ref, low_ref, high_ref, half, head):
    rim = low_ref.shape[0] // 2
    rows = slice(half * rim, (half + 1) * rim)
    return jnp.concatenate(
        [low_ref[rows, lanes(head)], own_ref[:, lanes(head)], high_ref[rows, lanes(head)]], 0
    )


def spatial_fwd_kernel(total_rows, breadth, first_ref, q_ref, k_ref, v_ref, low_ref, high_ref, s_ref):
    queries = q_ref.shape[0]
    keys = queries + low_ref.shape[0]
    allowed = window_mask(first_ref[0], total_rows, breadth, keys, queries)
    for head in range(q_ref.shape[1] // HEAD_DIM):
        key = window_of(k_ref, low_ref, high_ref, 0, head)
        value = window_of(v_ref, low_ref, high_ref, 1, head)
        scores = jnp.where(allowed, dot(key, q_ref[:, lanes(head)], NT), NEG_FILL)
        weights = softmax_columns(scores).astype(BF16)
        s_ref[:, :, lanes(head)] = chunked(dot(weights, value, TN), s_ref.shape[0]).astype(BF16)


def spatial_bwd_kernel(
    total_rows, breadth, first_ref, q_ref, k_ref, v_ref, low_ref, high_ref, g_ref,
    qs_ref, ks_ref, vs_ref, to_low_ref, to_high_ref,
):
    queries = q_ref.shape[0]
    rim = low_ref.shape[0] // 2
    keys = queries + 2 * rim
    allowed = window_mask(first_ref[0], total_rows, breadth, keys, queries)
    for head in range(q_ref.shape[1] // HEAD_DIM):
        at = lanes(head)
        query = q_ref[:, at]
        key = window_of(k_ref, low_ref, high_ref, 0, head)
        value = window_of(v_ref, low_ref, high_ref, 1, head)
        grad = flat_rows(g_ref[:, :, at]).astype(BF16)
        probs = softmax_columns(jnp.where(allowed, dot(key, query, NT), NEG_FILL))
        weights = probs.astype(BF16)
        prob_grad = dot(value, grad, NT)
        grad_dot = jnp.sum(weights.astype(F32) * prob_grad, 0, keepdims=True)
        score_grad = (probs * (prob_grad - grad_dot)).astype(BF16)
        qs_ref[:, at] = dot(score_grad, key, TN) * SCALING
        key_wide = dot(score_grad, query, NN) * SCALING
        value_wide = dot(weights, grad, NN)
        ks_ref[:, at] = key_wide[rim : rim + queries]
        vs_ref[:, at] = value_wide[rim : rim + queries]
        to_low_ref[:rim, at] = key_wide[:rim].astype(BF16)
        to_low_ref[rim:, at] = value_wide[:rim].astype(BF16)
        to_high_ref[:rim, at] = key_wide[rim + queries :].astype(BF16)
        to_high_ref[rim:, at] = value_wide[rim + queries :].astype(BF16)


def same_position(rows, spots):
    left = lax.broadcasted_iota(jnp.int32, (rows, rows), 0)
    right = lax.broadcasted_iota(jnp.int32, (rows, rows), 1)
    return left % spots == right % spots


def temporal_scores_kernel(q_ref, k_ref, g_ref, sent_ref, grad_ref, probs_ref):
    del sent_ref
    frames, spots = q_ref.shape[0], q_ref.shape[1]
    same = same_position(frames * spots, spots)
    for head in range(q_ref.shape[2] // HEAD_DIM):
        at = lanes(head)
        query = flat_rows(q_ref[:, :, at]).astype(BF16)
        key = flat_rows(k_ref[:, :, at]).astype(BF16)
        grad = flat_rows(g_ref[:, :, at]).astype(BF16)
        probs = softmax_columns(jnp.where(same, dot(key, query, NT), NEG_FILL))
        probs_ref[head] = probs
        grad_ref[:, :, at] = chunked(dot(probs.astype(BF16), grad, NN), frames).astype(BF16)


def temporal_grads_kernel(q_ref, k_ref, g_ref, s_ref, probs_ref, out_ref):
    frames = q_ref.shape[0]
    width = q_ref.shape[2]
    for head in range(width // HEAD_DIM):
        at = lanes(head)
        query = flat_rows(q_ref[:, :, at]).astype(BF16)
        key = flat_rows(k_ref[:, :, at]).astype(BF16)
        grad = flat_rows(g_ref[:, :, at]).astype(BF16)
        spatial = flat_rows(s_ref[:, :, at]).astype(BF16)
        probs = probs_ref[head]
        weights = probs.astype(BF16)
        prob_grad = dot(spatial, grad, NT)
        grad_dot = jnp.sum(weights.astype(F32) * prob_grad, 0, keepdims=True)
        score_grad = (probs * (prob_grad - grad_dot)).astype(BF16)
        time_out = dot(weights, spatial, TN)
        query_part = dot(score_grad, key, TN) * SCALING
        key_part = dot(score_grad, query, NN) * SCALING
        for place, part in enumerate((time_out, query_part, key_part)):
            first = place * width + head * HEAD_DIM
            out_ref[:, :, first : first + HEAD_DIM] = chunked(part, frames).astype(BF16)


def rim_add_kernel(ks_ref, vs_ref, from_low_ref, from_high_ref, key_ref, value_ref):
    rim = from_low_ref.shape[0] // 2
    rows = ks_ref.shape[0]
    for sum_ref, out_ref, half in ((ks_ref, key_ref, 0), (vs_ref, value_ref, 1)):
        part = slice(half * rim, (half + 1) * rim)
        out_ref[:rim] = (sum_ref[:rim] + from_low_ref[part].astype(F32)).astype(out_ref.dtype)
        out_ref[rim : rows - rim] = sum_ref[rim : rows - rim].astype(out_ref.dtype)
        out_ref[rows - rim :] = (sum_ref[rows - rim :] + from_high_ref[part].astype(F32)).astype(
            out_ref.dtype
        )


def last_sum_kernel(back_ref, qs_ref, ks_ref, out_ref, query_ref, key_ref):
    for piece in range(back_ref.shape[2] // (3 * TIME_HEADS * HEAD_DIM)):
        width = TIME_HEADS * HEAD_DIM
        first = piece * 3 * width
        at = slice(piece * width, (piece + 1) * width)
        out_ref[:, at] = flat_rows(back_ref[:, :, first : first + width]).astype(BF16)
        first = first + width
        query_ref[:, at] = (flat_rows(back_ref[:, :, first : first + width]) + qs_ref[:, at]).astype(BF16)
        first = first + width
        key_ref[:, at] = (flat_rows(back_ref[:, :, first : first + width]) + ks_ref[:, at]).astype(BF16)


def exchange(chunks):
    return lax.all_to_all(chunks, "tm", split_axis=0, concat_axis=0, tiled=True)


def on_device(queries, key_states, value_states, out_grad):
    band_rows, breadth, channels = queries.shape[1:]
    tokens = band_rows * breadth
    rim = RADIUS * breadth
    parts = lax.axis_size("tm")
    bands = lax.axis_size("rows")
    spots = tokens // parts
    first_row = (lax.axis_index("rows") * band_rows).astype(jnp.int32).reshape(1)
    total_rows = bands * band_rows
    upward = [(i, i + 1) for i in range(bands - 1)]
    downward = [(i + 1, i) for i in range(bands - 1)]

    def chunks_of(tensor):
        return tensor.reshape(parts, spots, channels)

    moved = exchange(
        jnp.concatenate([chunks_of(queries), chunks_of(key_states), chunks_of(out_grad)], 2)
    )

    query, key, value = (
        tensor.reshape(tokens, channels) for tensor in (queries, key_states, value_states)
    )
    low = lax.ppermute(jnp.concatenate([key[tokens - rim :], value[tokens - rim :]], 0), "rows", upward)
    high = lax.ppermute(jnp.concatenate([key[:rim], value[:rim]], 0), "rows", downward)

    scalar = pl.BlockSpec(memory_space=pltpu.SMEM)

    def rows_block(rows, heads):
        return pl.BlockSpec((rows, heads * HEAD_DIM), lambda i: (0, i))

    def chunk_block(heads, offset, stride=1):
        return pl.BlockSpec((parts, spots, heads * HEAD_DIM), lambda i: (0, 0, i * stride + offset))

    def band_specs(heads):
        own = rows_block(tokens, heads)
        return [scalar, own, own, own, rows_block(2 * rim, heads), rows_block(2 * rim, heads)]

    sent = call(
        functools.partial(spatial_fwd_kernel, total_rows, breadth),
        HEADS // FWD_HEADS,
        band_specs(FWD_HEADS),
        chunk_block(FWD_HEADS, 0),
        jax.ShapeDtypeStruct((parts, spots, 2 * channels), BF16),
    )(first_row, query, key, value, low, high)

    count = HEADS // SCORE_HEADS
    sent, probs = call(
        temporal_scores_kernel,
        count,
        [chunk_block(SCORE_HEADS, place * count) for place in range(3)]
        + [pl.BlockSpec(memory_space=pl.ANY)],
        [
            chunk_block(SCORE_HEADS, count),
            pl.BlockSpec((SCORE_HEADS, tokens, tokens), lambda i: (i, 0, 0)),
        ],
        [
            jax.ShapeDtypeStruct(sent.shape, BF16),
            jax.ShapeDtypeStruct((HEADS, tokens, tokens), F32),
        ],
        input_output_aliases={3: 0},
    )(moved, moved, moved, sent)
    both = exchange(sent)

    count = HEADS // TIME_HEADS
    parts_out = call(
        temporal_grads_kernel,
        count,
        [chunk_block(TIME_HEADS, place * count) for place in range(3)]
        + [
            chunk_block(TIME_HEADS, 0),
            pl.BlockSpec((TIME_HEADS, tokens, tokens), lambda i: (i, 0, 0)),
        ],
        chunk_block(3 * TIME_HEADS, 0),
        jax.ShapeDtypeStruct((parts, spots, 3 * channels), BF16),
    )(moved, moved, moved, both, probs)
    parts_out, both = lax.optimization_barrier((parts_out, both))
    back = exchange(parts_out)

    count = HEADS // BWD_HEADS
    own = rows_block(tokens, BWD_HEADS)
    whole = jax.ShapeDtypeStruct((tokens, channels), F32)
    rims = jax.ShapeDtypeStruct((2 * rim, channels), BF16)
    qs, ks, vs, to_low, to_high = call(
        functools.partial(spatial_bwd_kernel, total_rows, breadth),
        count,
        band_specs(BWD_HEADS) + [chunk_block(BWD_HEADS, count)],
        [own, own, own, rows_block(2 * rim, BWD_HEADS), rows_block(2 * rim, BWD_HEADS)],
        [whole, whole, whole, rims, rims],
    )(first_row, query, key, value, low, high, both)
    from_high = lax.ppermute(to_low, "rows", downward)
    from_low = lax.ppermute(to_high, "rows", upward)
    final = jax.ShapeDtypeStruct((tokens, channels), BF16)
    own = rows_block(tokens, RIM_HEADS)
    ks, value_grad = call(
        rim_add_kernel,
        HEADS // RIM_HEADS,
        [own, own, rows_block(2 * rim, RIM_HEADS), rows_block(2 * rim, RIM_HEADS)],
        [own, own],
        [whole, final],
    )(ks, vs, from_low, from_high)

    own = rows_block(tokens, LAST_HEADS * 2)
    temporal_out, query_grad, key_grad = call(
        last_sum_kernel,
        HEADS // (LAST_HEADS * 2),
        [chunk_block(3 * LAST_HEADS * 2, 0), own, own],
        [own, own, own],
        [final, final, final],
    )(back, qs, ks)
    return tuple(
        tensor.reshape(queries.shape) for tensor in (temporal_out, query_grad, key_grad, value_grad)
    )


def solution(mesh):
    placed = P("tm", "rows", None, None)
    return jax.shard_map(
        on_device,
        mesh=mesh,
        in_specs=(placed,) * 4,
        out_specs=(placed,) * 4,
        check_vma=False,
    )
```

```python
import functools

import jax
import jax.numpy as jnp
from jax import lax
from jax.experimental import pallas as pl
from jax.experimental.pallas import tpu as pltpu
from jax.sharding import PartitionSpec as P

HEADS = 24
HEAD_DIM = 128
RADIUS = 3
SCALING = HEAD_DIM ** (-0.5)
NEG_FILL = -1e30
BF16 = jnp.bfloat16
F32 = jnp.float32

FWD_HEADS = 4
SCORE_HEADS = 8
TIME_HEADS = 8
BWD_HEADS = 4
RIM_HEADS = 8
PIECES = 4

NT = (((1,), (1,)), ((), ()))
NN = (((1,), (0,)), ((), ()))
TN = (((0,), (0,)), ((), ()))


def dot(left, right, dims):
    return lax.dot_general(left, right, dims, preferred_element_type=F32)


def lanes(head):
    return slice(head * HEAD_DIM, (head + 1) * HEAD_DIM)


def flat_rows(chunks):
    wide = chunks.astype(F32)
    return wide.reshape(wide.shape[0] * wide.shape[1], wide.shape[2])


def head_rows(ref, head):
    return flat_rows(ref[:, :, lanes(head)]).astype(BF16)


def chunked(matrix, chunks):
    return matrix.reshape(chunks, matrix.shape[0] // chunks, matrix.shape[1])


def softmax_columns(scores):
    peak = jnp.max(scores, 0, keepdims=True)
    grown = jnp.exp((scores - peak) * SCALING)
    return grown * (1.0 / jnp.sum(grown, 0, keepdims=True))


params = pltpu.CompilerParams(vmem_limit_bytes=16 * 1024 * 1024)


def call(kernel, grid, in_specs, out_specs, out_shape, **more):
    return pl.pallas_call(
        kernel,
        grid=(grid,),
        in_specs=in_specs,
        out_specs=out_specs,
        out_shape=out_shape,
        compiler_params=params,
        **more,
    )


def window_mask(first_row, total_rows, breadth, keys, queries, reach=RADIUS):
    key = lax.broadcasted_iota(jnp.int32, (keys, queries), 0)
    query = lax.broadcasted_iota(jnp.int32, (keys, queries), 1)
    row_step = key // breadth - reach - query // breadth
    col_step = key % breadth - query % breadth
    key_row = first_row - reach + key // breadth
    return (
        (jnp.abs(row_step) <= RADIUS)
        & (jnp.abs(col_step) <= RADIUS)
        & (key_row >= 0)
        & (key_row < total_rows)
    )


def window_of(own_ref, low_ref, high_ref, half, head):
    at = lanes(head)
    return jnp.concatenate([low_ref[half, :, at], own_ref[:, at], high_ref[half, :, at]], 0)


def spatial_fwd_kernel(total_rows, breadth, first_ref, q_ref, k_ref, v_ref, low_ref, high_ref, s_ref):
    queries = q_ref.shape[0]
    keys = queries + 2 * low_ref.shape[1]
    allowed = window_mask(first_ref[0], total_rows, breadth, keys, queries)
    heads = range(q_ref.shape[1] // HEAD_DIM)
    scores = [
        dot(window_of(k_ref, low_ref, high_ref, 0, head), q_ref[:, lanes(head)], NT) for head in heads
    ]
    weights = [softmax_columns(jnp.where(allowed, part, NEG_FILL)).astype(BF16) for part in scores]
    outs = [dot(weights[head], window_of(v_ref, low_ref, high_ref, 1, head), TN) for head in heads]
    for head in heads:
        s_ref[:, :, lanes(head)] = chunked(outs[head], s_ref.shape[0]).astype(BF16)


def spatial_bwd_kernel(
    total_rows, breadth, first_ref, q_ref, k_ref, v_ref, low_ref, high_ref, g_ref,
    qs_ref, ks_ref, vs_ref, to_low_ref, to_high_ref,
):
    queries = q_ref.shape[0]
    rim = low_ref.shape[1]
    keys = queries + 2 * rim
    allowed = window_mask(first_ref[0], total_rows, breadth, keys, queries)
    heads = range(q_ref.shape[1] // HEAD_DIM)
    scores = [
        dot(window_of(k_ref, low_ref, high_ref, 0, head), q_ref[:, lanes(head)], NT) for head in heads
    ]
    grads = [head_rows(g_ref, head) for head in heads]
    prob_grads = [
        dot(window_of(v_ref, low_ref, high_ref, 1, head), grads[head], NT) for head in heads
    ]
    weights, score_grads = [], []
    for head in heads:
        probs = softmax_columns(jnp.where(allowed, scores[head], NEG_FILL))
        weights.append(probs.astype(BF16))
        grad_dot = jnp.sum(weights[head].astype(F32) * prob_grads[head], 0, keepdims=True)
        score_grads.append((probs * (prob_grads[head] - grad_dot)).astype(BF16))
    values = [dot(weights[head], grads[head], NN) for head in heads]
    keys = [dot(score_grads[head], q_ref[:, lanes(head)], NN) * SCALING for head in heads]
    for wide, own_ref, half in (
        (keys, ks_ref, 0),
        (values, vs_ref, 1),
    ):
        for head in heads:
            at = lanes(head)
            own_ref[:, at] = wide[head][rim : rim + queries]
            to_low_ref[half, :, at] = wide[head][:rim].astype(BF16)
            to_high_ref[half, :, at] = wide[head][rim + queries :].astype(BF16)
    for head in heads:
        key = window_of(k_ref, low_ref, high_ref, 0, head)
        qs_ref[:, lanes(head)] = dot(score_grads[head], key, TN) * SCALING


def same_position(rows, spots):
    left = lax.broadcasted_iota(jnp.int32, (rows, rows), 0)
    right = lax.broadcasted_iota(jnp.int32, (rows, rows), 1)
    return left % spots == right % spots


def temporal_scores_kernel(q_ref, k_ref, g_ref, sent_ref, grad_ref, probs_ref):
    del sent_ref
    frames, spots = q_ref.shape[0], q_ref.shape[1]
    same = same_position(frames * spots, spots)
    heads = range(q_ref.shape[2] // HEAD_DIM)
    scores = [dot(head_rows(k_ref, head), head_rows(q_ref, head), NT) for head in heads]
    probs = [softmax_columns(jnp.where(same, part, NEG_FILL)) for part in scores]
    grads = [dot(probs[head].astype(BF16), head_rows(g_ref, head), NN) for head in heads]
    for head in heads:
        probs_ref[head] = probs[head]
    for head in heads:
        grad_ref[:, :, lanes(head)] = chunked(grads[head], frames).astype(BF16)


def temporal_grads_kernel(q_ref, k_ref, g_ref, s_ref, probs_ref, out_ref):
    frames = q_ref.shape[0]
    width = q_ref.shape[2]
    heads = range(width // HEAD_DIM)
    spatial = [head_rows(s_ref, head) for head in heads]
    prob_grads = [dot(spatial[head], head_rows(g_ref, head), NT) for head in heads]
    outs = [dot(probs_ref[head].astype(BF16), spatial[head], TN) for head in heads]
    score_grads = []
    for head in heads:
        probs = probs_ref[head]
        weights = probs.astype(BF16).astype(F32)
        grad_dot = jnp.sum(weights * prob_grads[head], 0, keepdims=True)
        score_grads.append((probs * (prob_grads[head] - grad_dot)).astype(BF16))
    query_parts = [dot(score_grads[head], head_rows(k_ref, head), TN) * SCALING for head in heads]
    key_parts = [dot(score_grads[head], head_rows(q_ref, head), NN) * SCALING for head in heads]
    for place, parts in enumerate((outs, query_parts, key_parts)):
        for head in heads:
            first = place * width + head * HEAD_DIM
            out_ref[:, :, first : first + HEAD_DIM] = chunked(parts[head], frames).astype(BF16)


def rims_kernel(k_first_ref, v_first_ref, k_last_ref, v_last_ref, to_low_ref, to_high_ref):
    to_low_ref[0] = k_first_ref[...]
    to_low_ref[1] = v_first_ref[...]
    to_high_ref[0] = k_last_ref[...]
    to_high_ref[1] = v_last_ref[...]


def started(source, target, sem):
    copy = pltpu.make_async_copy(source, target, sem)
    copy.start()
    return copy


def join_kernel(*refs):
    sources, (joined_ref, held, load_sems, store_sems) = refs[:-4], refs[-4:]
    pieces = load_sems.shape[0]
    chunks, width = joined_ref.shape[0] // pieces, sources[0].shape[2]
    loads = []
    for piece in range(pieces):
        rows = slice(piece * chunks, (piece + 1) * chunks)
        loads.append(
            [
                started(
                    source.at[rows],
                    held.at[rows, :, place * width : (place + 1) * width],
                    load_sems.at[piece, place],
                )
                for place, source in enumerate(sources)
            ]
        )
    stores = []
    for piece in range(pieces):
        rows = slice(piece * chunks, (piece + 1) * chunks)
        for load in loads[piece]:
            load.wait()
        stores.append(started(held.at[rows], joined_ref.at[rows], store_sems.at[piece]))
    for store in stores:
        store.wait()


def rim_add_kernel(ks_ref, vs_ref, from_low_ref, from_high_ref, key_ref, value_ref):
    rim = from_low_ref.shape[1]
    rows = ks_ref.shape[0]
    for half, (sum_ref, out_ref) in enumerate(((ks_ref, key_ref), (vs_ref, value_ref))):
        out_ref[:rim] = (sum_ref[:rim] + from_low_ref[half].astype(F32)).astype(out_ref.dtype)
        out_ref[rim : rows - rim] = sum_ref[rim : rows - rim].astype(out_ref.dtype)
        out_ref[rows - rim :] = (sum_ref[rows - rim :] + from_high_ref[half].astype(F32)).astype(
            out_ref.dtype
        )


def last_sum_kernel(back_ref, qs_ref, ks_ref, *refs):
    outs, (back, qs, ks), results, (load_sems, store_sems) = refs[:3], refs[3:6], refs[6:9], refs[9:]
    pieces = load_sems.shape[0]
    chunks, rows = back.shape[0] // pieces, qs.shape[0] // pieces
    width = TIME_HEADS * HEAD_DIM
    loads, stores = [], []
    for piece in range(pieces):
        some = slice(piece * chunks, (piece + 1) * chunks)
        at = slice(piece * rows, (piece + 1) * rows)
        pairs = ((back_ref.at[some], back.at[some]), (qs_ref.at[at], qs.at[at]), (ks_ref.at[at], ks.at[at]))
        loads.append(
            [started(*pair, load_sems.at[piece, place]) for place, pair in enumerate(pairs)]
        )
    for piece in range(pieces):
        for load in loads[piece]:
            load.wait()
        some = slice(piece * chunks, (piece + 1) * chunks)
        at = slice(piece * rows, (piece + 1) * rows)
        for group in range(HEADS // TIME_HEADS):
            to = slice(group * width, (group + 1) * width)
            parts = [
                flat_rows(back[some, :, (group * 3 + place) * width : (group * 3 + place + 1) * width])
                for place in range(3)
            ]
            results[0][at, to] = parts[0].astype(BF16)
            results[1][at, to] = (parts[1] + qs[at, to]).astype(BF16)
            results[2][at, to] = (parts[2] + ks[at, to]).astype(BF16)
        for place in range(3):
            stores.append(
                started(results[place].at[at], outs[place].at[at], store_sems.at[piece, place])
            )
    for store in stores:
        store.wait()


def in_hbm(tensor):
    return pltpu.with_memory_space_constraint(tensor, pltpu.HBM)


def exchange(chunks):
    return lax.all_to_all(chunks, "tm", split_axis=0, concat_axis=0, tiled=True)


def on_device(queries, key_states, value_states, out_grad):
    band_rows, breadth, channels = queries.shape[1:]
    tokens = band_rows * breadth
    rim = RADIUS * breadth
    parts = lax.axis_size("tm")
    bands = lax.axis_size("rows")
    spots = tokens // parts
    band = lax.axis_index("rows").astype(jnp.int32)
    first_row = (band * band_rows).reshape(1)
    total_rows = bands * band_rows
    upward = [(i, i + 1) for i in range(bands - 1)]
    downward = [(i + 1, i) for i in range(bands - 1)]

    scalar = pl.BlockSpec(memory_space=pltpu.SMEM)
    anywhere = pl.BlockSpec(memory_space=pl.ANY)

    def rows_block(rows, heads):
        return pl.BlockSpec((rows, heads * HEAD_DIM), lambda i: (0, i))

    def rims_block(heads):
        return pl.BlockSpec((2, rim, heads * HEAD_DIM), lambda i: (0, 0, i))

    def chunk_block(heads, offset, stride=1):
        return pl.BlockSpec((parts, spots, heads * HEAD_DIM), lambda i: (0, 0, i * stride + offset))

    query, key, value = (
        tensor.reshape(tokens, channels) for tensor in (queries, key_states, value_states)
    )
    rims = jax.ShapeDtypeStruct((2, rim, channels), BF16)
    first_rows = pl.BlockSpec((breadth, channels), lambda i: (i, 0))
    last_rows = pl.BlockSpec((breadth, channels), lambda i: (i + band_rows - RADIUS, 0))
    rim_rows = pl.BlockSpec((2, breadth, channels), lambda i: (0, i, 0))
    to_low, to_high = call(
        rims_kernel,
        RADIUS,
        [first_rows, first_rows, last_rows, last_rows],
        [rim_rows, rim_rows],
        [pltpu.HBM(rims.shape, BF16)] * 2,
    )(*map(in_hbm, (key, value, key, value)))
    low = lax.ppermute(to_high, "rows", upward)
    high = lax.ppermute(to_low, "rows", downward)

    joined_shape = (parts, spots, 3 * channels)
    joined = pl.pallas_call(
        join_kernel,
        in_specs=[anywhere] * 3,
        out_specs=anywhere,
        out_shape=pltpu.HBM(joined_shape, BF16),
        scratch_shapes=[
            pltpu.VMEM(joined_shape, BF16),
            pltpu.SemaphoreType.DMA((PIECES, 3)),
            pltpu.SemaphoreType.DMA((PIECES,)),
        ],
        compiler_params=params,
    )(*(in_hbm(tensor.reshape(parts, spots, channels)) for tensor in (queries, key_states, out_grad)))
    moved = exchange(joined)

    own = rows_block(tokens, FWD_HEADS)
    sent = call(
        functools.partial(spatial_fwd_kernel, total_rows, breadth),
        HEADS // FWD_HEADS,
        [scalar, own, own, own, rims_block(FWD_HEADS), rims_block(FWD_HEADS)],
        chunk_block(FWD_HEADS, 0),
        pltpu.HBM((parts, spots, 2 * channels), BF16),
    )(first_row, query, key, value, low, high)

    count = HEADS // SCORE_HEADS
    sent, probs = call(
        temporal_scores_kernel,
        count,
        [chunk_block(SCORE_HEADS, place * count) for place in range(3)]
        + [anywhere],
        [
            chunk_block(SCORE_HEADS, count),
            pl.BlockSpec((SCORE_HEADS, tokens, tokens), lambda i: (i, 0, 0)),
        ],
        [
            pltpu.HBM(sent.shape, BF16),
            jax.ShapeDtypeStruct((HEADS, tokens, tokens), F32),
        ],
        input_output_aliases={3: 0},
    )(moved, moved, moved, sent)
    both = in_hbm(exchange(sent))

    count = HEADS // TIME_HEADS
    parts_out = call(
        temporal_grads_kernel,
        count,
        [chunk_block(TIME_HEADS, place * count) for place in range(3)]
        + [
            chunk_block(TIME_HEADS, 0),
            pl.BlockSpec((TIME_HEADS, tokens, tokens), lambda i: (i, 0, 0)),
        ],
        chunk_block(3 * TIME_HEADS, 0),
        pltpu.HBM((parts, spots, 3 * channels), BF16),
    )(moved, moved, moved, both, probs)
    parts_out, both = lax.optimization_barrier((parts_out, both))
    back = exchange(parts_out)

    count = HEADS // BWD_HEADS
    own = rows_block(tokens, BWD_HEADS)
    whole = jax.ShapeDtypeStruct((tokens, channels), F32)
    qs, ks, vs, to_low, to_high = call(
        functools.partial(spatial_bwd_kernel, total_rows, breadth),
        count,
        [scalar, own, own, own, rims_block(BWD_HEADS), rims_block(BWD_HEADS), chunk_block(BWD_HEADS, count)],
        [own, own, own, rims_block(BWD_HEADS), rims_block(BWD_HEADS)],
        [pltpu.HBM((tokens, channels), F32), whole, whole, rims, rims],
    )(first_row, query, key, value, low, high, in_hbm(both))
    from_high = lax.ppermute(to_low, "rows", downward)
    from_low = lax.ppermute(to_high, "rows", upward)
    final = jax.ShapeDtypeStruct((tokens, channels), BF16)
    own = rows_block(tokens, RIM_HEADS)
    ks, value_grad = call(
        rim_add_kernel,
        HEADS // RIM_HEADS,
        [own, own, rims_block(RIM_HEADS), rims_block(RIM_HEADS)],
        [own, own],
        [pltpu.HBM((tokens, channels), F32), final],
    )(ks, vs, from_low, from_high)

    temporal_out, query_grad, key_grad = pl.pallas_call(
        last_sum_kernel,
        in_specs=[anywhere] * 3,
        out_specs=[anywhere] * 3,
        out_shape=[pltpu.HBM((tokens, channels), BF16)] * 3,
        scratch_shapes=[pltpu.VMEM(joined_shape, BF16)]
        + [pltpu.VMEM((tokens, channels), F32)] * 2
        + [pltpu.VMEM((tokens, channels), BF16)] * 3
        + [pltpu.SemaphoreType.DMA((PIECES, 3))] * 2,
        compiler_params=params,
    )(back, in_hbm(qs), in_hbm(ks))
    return tuple(
        tensor.reshape(queries.shape) for tensor in (temporal_out, query_grad, key_grad, value_grad)
    )


def solution(mesh):
    placed = P("tm", "rows", None, None)
    return jax.shard_map(
        on_device,
        mesh=mesh,
        in_specs=(placed,) * 4,
        out_specs=(placed,) * 4,
        check_vma=False,
    )
```

```python
import functools

import jax
import jax.numpy as jnp
from jax import lax
from jax.experimental import pallas as pl
from jax.experimental.pallas import tpu as pltpu
from jax.sharding import PartitionSpec as P

HEADS = 24
HEAD_DIM = 128
RADIUS = 3
SCALING = HEAD_DIM ** (-0.5)
NEG_FILL = -1e30
BF16 = jnp.bfloat16
F32 = jnp.float32

FWD_HEADS = 4
TIME_HEADS = 8
BWD_HEADS = 4
RIM_HEADS = 8
PIECES = 4

NT = (((1,), (1,)), ((), ()))
NN = (((1,), (0,)), ((), ()))
TN = (((0,), (0,)), ((), ()))


def dot(left, right, dims):
    return lax.dot_general(left, right, dims, preferred_element_type=F32)


def lanes(head):
    return slice(head * HEAD_DIM, (head + 1) * HEAD_DIM)


def flat_rows(chunks):
    wide = chunks.astype(F32)
    return wide.reshape(wide.shape[0] * wide.shape[1], wide.shape[2])


def head_rows(ref, head):
    return flat_rows(ref[:, :, lanes(head)]).astype(BF16)


def chunked(matrix, chunks):
    return matrix.reshape(chunks, matrix.shape[0] // chunks, matrix.shape[1])


def softmax_columns(scores):
    peak = jnp.max(scores, 0, keepdims=True)
    grown = jnp.exp((scores - peak) * SCALING)
    return grown * (1.0 / jnp.sum(grown, 0, keepdims=True))


params = pltpu.CompilerParams(vmem_limit_bytes=16 * 1024 * 1024)


def call(kernel, grid, in_specs, out_specs, out_shape, **more):
    return pl.pallas_call(
        kernel,
        grid=(grid,),
        in_specs=in_specs,
        out_specs=out_specs,
        out_shape=out_shape,
        compiler_params=params,
        **more,
    )


def window_mask(first_row, total_rows, breadth, keys, queries, reach=RADIUS):
    key = lax.broadcasted_iota(jnp.int32, (keys, queries), 0)
    query = lax.broadcasted_iota(jnp.int32, (keys, queries), 1)
    row_step = key // breadth - reach - query // breadth
    col_step = key % breadth - query % breadth
    key_row = first_row - reach + key // breadth
    return (
        (jnp.abs(row_step) <= RADIUS)
        & (jnp.abs(col_step) <= RADIUS)
        & (key_row >= 0)
        & (key_row < total_rows)
    )


def window_of(own_ref, low_ref, high_ref, half, head):
    at = lanes(head)
    return jnp.concatenate([low_ref[half, :, at], own_ref[:, at], high_ref[half, :, at]], 0)


def spatial_fwd_kernel(total_rows, breadth, first_ref, q_ref, k_ref, v_ref, low_ref, high_ref, s_ref):
    queries = q_ref.shape[0]
    keys = queries + 2 * low_ref.shape[1]
    allowed = window_mask(first_ref[0], total_rows, breadth, keys, queries)
    heads = range(q_ref.shape[1] // HEAD_DIM)
    scores = [
        dot(window_of(k_ref, low_ref, high_ref, 0, head), q_ref[:, lanes(head)], NT) for head in heads
    ]
    weights = [softmax_columns(jnp.where(allowed, part, NEG_FILL)).astype(BF16) for part in scores]
    outs = [dot(weights[head], window_of(v_ref, low_ref, high_ref, 1, head), TN) for head in heads]
    for head in heads:
        s_ref[:, :, lanes(head)] = chunked(outs[head], s_ref.shape[0]).astype(BF16)


def spatial_bwd_kernel(
    total_rows, breadth, first_ref, q_ref, k_ref, v_ref, low_ref, high_ref, g_ref,
    qs_ref, ks_ref, vs_ref, to_low_ref, to_high_ref,
):
    queries = q_ref.shape[0]
    rim = low_ref.shape[1]
    keys = queries + 2 * rim
    allowed = window_mask(first_ref[0], total_rows, breadth, keys, queries)
    heads = range(q_ref.shape[1] // HEAD_DIM)
    scores = [
        dot(window_of(k_ref, low_ref, high_ref, 0, head), q_ref[:, lanes(head)], NT) for head in heads
    ]
    grads = [head_rows(g_ref, head) for head in heads]
    prob_grads = [
        dot(window_of(v_ref, low_ref, high_ref, 1, head), grads[head], NT) for head in heads
    ]
    weights, score_grads = [], []
    for head in heads:
        probs = softmax_columns(jnp.where(allowed, scores[head], NEG_FILL))
        weights.append(probs.astype(BF16))
        grad_dot = jnp.sum(weights[head].astype(F32) * prob_grads[head], 0, keepdims=True)
        score_grads.append((probs * (prob_grads[head] - grad_dot)).astype(BF16))
    values = [dot(weights[head], grads[head], NN) for head in heads]
    keys = [dot(score_grads[head], q_ref[:, lanes(head)], NN) * SCALING for head in heads]
    for wide, own_ref, half in (
        (keys, ks_ref, 0),
        (values, vs_ref, 1),
    ):
        for head in heads:
            at = lanes(head)
            own_ref[:, at] = wide[head][rim : rim + queries]
            to_low_ref[half, :, at] = wide[head][:rim].astype(BF16)
            to_high_ref[half, :, at] = wide[head][rim + queries :].astype(BF16)
    for head in heads:
        key = window_of(k_ref, low_ref, high_ref, 0, head)
        query_sum = dot(score_grads[head], key, TN) * SCALING
        qs_ref[:, :, lanes(head)] = chunked(query_sum, qs_ref.shape[0]).astype(BF16)


def same_position(rows, spots):
    left = lax.broadcasted_iota(jnp.int32, (rows, rows), 0)
    right = lax.broadcasted_iota(jnp.int32, (rows, rows), 1)
    return left % spots == right % spots


def temporal_scores_kernel(moved_ref, begun_ref, sent_ref, probs_ref, held, sems):
    del begun_ref
    frames, spots = moved_ref.shape[0], moved_ref.shape[1]
    channels = HEADS * HEAD_DIM
    same = same_position(frames * spots, spots)
    stores = []
    for group in range(HEADS // TIME_HEADS):
        heads = range(group * TIME_HEADS, (group + 1) * TIME_HEADS)
        scores = [
            dot(head_rows(moved_ref, HEADS + head), head_rows(moved_ref, head), NT) for head in heads
        ]
        probs = [softmax_columns(jnp.where(same, part, NEG_FILL)) for part in scores]
        grads = [
            dot(part.astype(BF16), head_rows(moved_ref, 2 * HEADS + head), NN)
            for part, head in zip(probs, heads)
        ]
        for part, head in zip(probs, heads):
            probs_ref[head] = part
        for part, head in zip(grads, heads):
            held[:, :, lanes(head)] = chunked(part, frames).astype(BF16)
        first, last = group * TIME_HEADS * HEAD_DIM, (group + 1) * TIME_HEADS * HEAD_DIM
        stores.append(
            started(
                held.at[:, :, first:last],
                sent_ref.at[:, :, channels + first : channels + last],
                sems.at[group],
            )
        )
    for store in stores:
        store.wait()


def temporal_grads_kernel(moved_ref, both_ref, probs_ref, out_ref, spatial_held, held, load_sems, store_sems):
    frames = moved_ref.shape[0]
    width = TIME_HEADS * HEAD_DIM
    groups = range(HEADS // TIME_HEADS)
    loads, stores = [], []
    for group in groups:
        at = slice(group * width, (group + 1) * width)
        loads.append(started(both_ref.at[:, :, at], spatial_held.at[:, :, at], load_sems.at[group]))
    for group in groups:
        heads = range(group * TIME_HEADS, (group + 1) * TIME_HEADS)
        loads[group].wait()
        spatial = [head_rows(spatial_held, head) for head in heads]
        prob_grads = [
            dot(part, head_rows(moved_ref, 2 * HEADS + head), NT) for part, head in zip(spatial, heads)
        ]
        outs = [dot(probs_ref[head].astype(BF16), part, TN) for part, head in zip(spatial, heads)]
        score_grads = []
        for prob_grad, head in zip(prob_grads, heads):
            probs = probs_ref[head]
            weights = probs.astype(BF16).astype(F32)
            grad_dot = jnp.sum(weights * prob_grad, 0, keepdims=True)
            score_grads.append((probs * (prob_grad - grad_dot)).astype(BF16))
        query_parts = [
            dot(part, head_rows(moved_ref, HEADS + head), TN) * SCALING
            for part, head in zip(score_grads, heads)
        ]
        key_parts = [
            dot(part, head_rows(moved_ref, head), NN) * SCALING for part, head in zip(score_grads, heads)
        ]
        for place, parts in enumerate((outs, query_parts, key_parts)):
            for step, part in enumerate(parts):
                first = (group * 3 + place) * width + step * HEAD_DIM
                held[:, :, first : first + HEAD_DIM] = chunked(part, frames).astype(BF16)
        at = slice(group * 3 * width, (group + 1) * 3 * width)
        stores.append(started(held.at[:, :, at], out_ref.at[:, :, at], store_sems.at[group]))
    for store in stores:
        store.wait()


def rims_kernel(k_first_ref, v_first_ref, k_last_ref, v_last_ref, to_low_ref, to_high_ref):
    to_low_ref[0] = k_first_ref[...]
    to_low_ref[1] = v_first_ref[...]
    to_high_ref[0] = k_last_ref[...]
    to_high_ref[1] = v_last_ref[...]


def started(source, target, sem):
    copy = pltpu.make_async_copy(source, target, sem)
    copy.start()
    return copy


def join_kernel(*refs):
    sources, (joined_ref, held, load_sems, store_sems) = refs[:-4], refs[-4:]
    pieces = load_sems.shape[0]
    chunks, width = joined_ref.shape[0] // pieces, sources[0].shape[2]
    loads = []
    for piece in range(pieces):
        rows = slice(piece * chunks, (piece + 1) * chunks)
        loads.append(
            [
                started(
                    source.at[rows],
                    held.at[rows, :, place * width : (place + 1) * width],
                    load_sems.at[piece, place],
                )
                for place, source in enumerate(sources)
            ]
        )
    stores = []
    for piece in range(pieces):
        rows = slice(piece * chunks, (piece + 1) * chunks)
        for load in loads[piece]:
            load.wait()
        stores.append(started(held.at[rows], joined_ref.at[rows], store_sems.at[piece]))
    for store in stores:
        store.wait()


def rim_add_kernel(ks_ref, vs_ref, from_low_ref, from_high_ref, key_ref, value_ref):
    rim = from_low_ref.shape[1]
    rows = ks_ref.shape[0]
    totals = [
        jnp.concatenate(
            [
                sum_ref[:rim] + from_low_ref[half].astype(F32),
                sum_ref[rim : rows - rim],
                sum_ref[rows - rim :] + from_high_ref[half].astype(F32),
            ],
            0,
        )
        for half, sum_ref in enumerate((ks_ref, vs_ref))
    ]
    key_ref[...] = chunked(totals[0], key_ref.shape[0]).astype(BF16)
    value_ref[...] = totals[1].astype(BF16)


def last_sum_kernel(back_ref, qs_ref, ks_ref, *refs):
    outs, (back, qs, ks), results, (load_sems, store_sems) = refs[:3], refs[3:6], refs[6:8], refs[8:]
    pieces = load_sems.shape[0]
    chunks = back.shape[0] // pieces
    width = TIME_HEADS * HEAD_DIM
    groups = range(HEADS // TIME_HEADS)
    pairs = ((back_ref, back), (qs_ref, qs), (ks_ref, ks))
    somes = [slice(piece * chunks, (piece + 1) * chunks) for piece in range(pieces)]
    loads, stores = [], []
    for piece, some in enumerate(somes):
        loads.append(
            [
                started(source.at[some], target.at[some], load_sems.at[piece, place])
                for place, (source, target) in enumerate(pairs)
            ]
        )
    for piece, some in enumerate(somes):
        for load in loads[piece]:
            load.wait()
        for group in groups:
            to = slice(group * width, (group + 1) * width)
            first = group * 3 * width
            stores.append(
                started(
                    back.at[some, :, first : first + width],
                    outs[0].at[some, :, to],
                    store_sems.at[piece, group],
                )
            )
            for place, (kept, result) in enumerate(((qs, results[0]), (ks, results[1]))):
                first += width
                part = back[some, :, first : first + width].astype(F32)
                result[some, :, to] = (part + kept[some, :, to].astype(F32)).astype(BF16)
        for place in range(2):
            stores.append(
                started(
                    results[place].at[some],
                    outs[1 + place].at[some],
                    store_sems.at[piece, len(groups) + place],
                )
            )
    for store in stores:
        store.wait()


def in_hbm(tensor):
    return pltpu.with_memory_space_constraint(tensor, pltpu.HBM)


def in_vmem(tensor):
    return pltpu.with_memory_space_constraint(tensor, pltpu.VMEM)


def exchange(chunks):
    return lax.all_to_all(chunks, "tm", split_axis=0, concat_axis=0, tiled=True)


def on_device(queries, key_states, value_states, out_grad):
    band_rows, breadth, channels = queries.shape[1:]
    tokens = band_rows * breadth
    rim = RADIUS * breadth
    parts = lax.axis_size("tm")
    bands = lax.axis_size("rows")
    spots = tokens // parts
    band = lax.axis_index("rows").astype(jnp.int32)
    first_row = (band * band_rows).reshape(1)
    total_rows = bands * band_rows
    upward = [(i, i + 1) for i in range(bands - 1)]
    downward = [(i + 1, i) for i in range(bands - 1)]

    scalar = pl.BlockSpec(memory_space=pltpu.SMEM)
    anywhere = pl.BlockSpec(memory_space=pl.ANY)

    def rows_block(rows, heads):
        return pl.BlockSpec((rows, heads * HEAD_DIM), lambda i: (0, i))

    def rims_block(heads):
        return pl.BlockSpec((2, rim, heads * HEAD_DIM), lambda i: (0, 0, i))

    def chunk_block(heads, offset, stride=1):
        return pl.BlockSpec((parts, spots, heads * HEAD_DIM), lambda i: (0, 0, i * stride + offset))

    query, key, value = (
        tensor.reshape(tokens, channels) for tensor in (queries, key_states, value_states)
    )
    rims = jax.ShapeDtypeStruct((2, rim, channels), BF16)
    first_rows = pl.BlockSpec((breadth, channels), lambda i: (i, 0))
    last_rows = pl.BlockSpec((breadth, channels), lambda i: (i + band_rows - RADIUS, 0))
    rim_rows = pl.BlockSpec((2, breadth, channels), lambda i: (0, i, 0))
    to_low, to_high = call(
        rims_kernel,
        RADIUS,
        [first_rows, first_rows, last_rows, last_rows],
        [rim_rows, rim_rows],
        [pltpu.HBM(rims.shape, BF16)] * 2,
    )(*map(in_hbm, (key, value, key, value)))
    low = lax.ppermute(to_high, "rows", upward)
    high = lax.ppermute(to_low, "rows", downward)

    joined_shape = (parts, spots, 3 * channels)
    joined = pl.pallas_call(
        join_kernel,
        in_specs=[anywhere] * 3,
        out_specs=anywhere,
        out_shape=pltpu.HBM(joined_shape, BF16),
        scratch_shapes=[
            pltpu.VMEM(joined_shape, BF16),
            pltpu.SemaphoreType.DMA((PIECES, 3)),
            pltpu.SemaphoreType.DMA((PIECES,)),
        ],
        compiler_params=params,
    )(*(in_hbm(tensor.reshape(parts, spots, channels)) for tensor in (queries, key_states, out_grad)))
    moved = exchange(joined)

    own = rows_block(tokens, FWD_HEADS)
    sent = call(
        functools.partial(spatial_fwd_kernel, total_rows, breadth),
        HEADS // FWD_HEADS,
        [scalar, own, own, own, rims_block(FWD_HEADS), rims_block(FWD_HEADS)],
        chunk_block(FWD_HEADS, 0),
        pltpu.HBM((parts, spots, 2 * channels), BF16),
    )(first_row, query, key, value, low, high)

    moved = in_vmem(moved)
    groups = HEADS // TIME_HEADS
    in_place = pl.BlockSpec(memory_space=pltpu.VMEM)
    sent, probs = pl.pallas_call(
        temporal_scores_kernel,
        in_specs=[in_place, anywhere],
        out_specs=[anywhere, in_place],
        out_shape=[pltpu.HBM(sent.shape, BF16), pltpu.VMEM((HEADS, tokens, tokens), F32)],
        scratch_shapes=[
            pltpu.VMEM((parts, spots, channels), BF16),
            pltpu.SemaphoreType.DMA((groups,)),
        ],
        input_output_aliases={1: 0},
        compiler_params=params,
    )(moved, in_hbm(sent))
    both = in_hbm(exchange(sent))

    parts_out = pl.pallas_call(
        temporal_grads_kernel,
        in_specs=[in_place, anywhere, in_place],
        out_specs=anywhere,
        out_shape=pltpu.HBM(joined_shape, BF16),
        scratch_shapes=[
            pltpu.VMEM((parts, spots, channels), BF16),
            pltpu.VMEM(joined_shape, BF16),
            pltpu.SemaphoreType.DMA((groups,)),
            pltpu.SemaphoreType.DMA((groups,)),
        ],
        compiler_params=params,
    )(moved, both, in_vmem(probs))
    parts_out, both = lax.optimization_barrier((parts_out, both))
    back = exchange(parts_out)

    count = HEADS // BWD_HEADS
    own = rows_block(tokens, BWD_HEADS)
    whole = jax.ShapeDtypeStruct((tokens, channels), F32)
    qs, ks, vs, to_low, to_high = call(
        functools.partial(spatial_bwd_kernel, total_rows, breadth),
        count,
        [scalar, own, own, own, rims_block(BWD_HEADS), rims_block(BWD_HEADS), chunk_block(BWD_HEADS, count)],
        [chunk_block(BWD_HEADS, 0), own, own, rims_block(BWD_HEADS), rims_block(BWD_HEADS)],
        [pltpu.HBM((parts, spots, channels), BF16), whole, whole, rims, rims],
    )(first_row, query, key, value, low, high, in_hbm(both))
    from_high = lax.ppermute(to_low, "rows", downward)
    from_low = lax.ppermute(to_high, "rows", upward)
    final = jax.ShapeDtypeStruct((tokens, channels), BF16)
    own = rows_block(tokens, RIM_HEADS)
    ks, value_grad = call(
        rim_add_kernel,
        HEADS // RIM_HEADS,
        [own, own, rims_block(RIM_HEADS), rims_block(RIM_HEADS)],
        [chunk_block(RIM_HEADS, 0), own],
        [pltpu.HBM((parts, spots, channels), BF16), final],
    )(ks, vs, from_low, from_high)

    temporal_out, query_grad, key_grad = pl.pallas_call(
        last_sum_kernel,
        in_specs=[anywhere] * 3,
        out_specs=[anywhere] * 3,
        out_shape=[pltpu.HBM((parts, spots, channels), BF16)] * 3,
        scratch_shapes=[pltpu.VMEM(joined_shape, BF16)]
        + [pltpu.VMEM((parts, spots, channels), BF16)] * 4
        + [pltpu.SemaphoreType.DMA((PIECES, 3)), pltpu.SemaphoreType.DMA((PIECES, groups + 2))],
        compiler_params=params,
    )(back, in_hbm(qs), in_hbm(ks))
    return tuple(
        tensor.reshape(queries.shape) for tensor in (temporal_out, query_grad, key_grad, value_grad)
    )


def solution(mesh):
    placed = P("tm", "rows", None, None)
    return jax.shard_map(
        on_device,
        mesh=mesh,
        in_specs=(placed,) * 4,
        out_specs=(placed,) * 4,
        check_vma=False,
    )
```

```python
import functools

import jax
import jax.numpy as jnp
from jax import lax
from jax.experimental import pallas as pl
from jax.experimental.pallas import tpu as pltpu
from jax.sharding import PartitionSpec as P

HEADS = 24
HEAD_DIM = 128
RADIUS = 3
SCALING = HEAD_DIM ** (-0.5)
NEG_FILL = -1e30
BF16 = jnp.bfloat16
F32 = jnp.float32

FWD_HEADS = 4
TIME_HEADS = 8
BWD_HEADS = 4
RIM_HEADS = 8
PIECES = 4

NT = (((1,), (1,)), ((), ()))
NN = (((1,), (0,)), ((), ()))
TN = (((0,), (0,)), ((), ()))


def dot(left, right, dims):
    return lax.dot_general(left, right, dims, preferred_element_type=F32)


def lanes(head):
    return slice(head * HEAD_DIM, (head + 1) * HEAD_DIM)


def flat_rows(chunks):
    wide = chunks.astype(F32)
    return wide.reshape(wide.shape[0] * wide.shape[1], wide.shape[2])


def head_rows(ref, head):
    return flat_rows(ref[:, :, lanes(head)]).astype(BF16)


def chunked(matrix, chunks):
    return matrix.reshape(chunks, matrix.shape[0] // chunks, matrix.shape[1])


def softmax_columns(scores):
    peak = jnp.max(scores, 0, keepdims=True)
    grown = jnp.exp((scores - peak) * SCALING)
    return grown * (1.0 / jnp.sum(grown, 0, keepdims=True))


params = pltpu.CompilerParams(vmem_limit_bytes=16 * 1024 * 1024)


def call(kernel, grid, in_specs, out_specs, out_shape, **more):
    return pl.pallas_call(
        kernel,
        grid=(grid,),
        in_specs=in_specs,
        out_specs=out_specs,
        out_shape=out_shape,
        compiler_params=params,
        **more,
    )


def window_mask(first_row, total_rows, breadth, keys, queries, reach=RADIUS):
    key = lax.broadcasted_iota(jnp.int32, (keys, queries), 0)
    query = lax.broadcasted_iota(jnp.int32, (keys, queries), 1)
    row_step = key // breadth - reach - query // breadth
    col_step = key % breadth - query % breadth
    key_row = first_row - reach + key // breadth
    return (
        (jnp.abs(row_step) <= RADIUS)
        & (jnp.abs(col_step) <= RADIUS)
        & (key_row >= 0)
        & (key_row < total_rows)
    )


def window_of(own_ref, low_ref, high_ref, half, head):
    at = lanes(head)
    return jnp.concatenate([low_ref[half, :, at], own_ref[:, at], high_ref[half, :, at]], 0)


def spatial_fwd_kernel(total_rows, breadth, first_ref, q_ref, k_ref, v_ref, low_ref, high_ref, s_ref):
    queries = q_ref.shape[0]
    keys = queries + 2 * low_ref.shape[1]
    allowed = window_mask(first_ref[0], total_rows, breadth, keys, queries)
    heads = range(q_ref.shape[1] // HEAD_DIM)
    scores = [
        dot(window_of(k_ref, low_ref, high_ref, 0, head), q_ref[:, lanes(head)], NT) for head in heads
    ]
    weights = [softmax_columns(jnp.where(allowed, part, NEG_FILL)).astype(BF16) for part in scores]
    outs = [dot(weights[head], window_of(v_ref, low_ref, high_ref, 1, head), TN) for head in heads]
    for head in heads:
        s_ref[:, :, lanes(head)] = chunked(outs[head], s_ref.shape[0]).astype(BF16)


def spatial_bwd_kernel(
    total_rows, breadth, first_ref, q_ref, k_ref, v_ref, low_ref, high_ref, g_ref,
    qs_ref, ks_ref, vs_ref, to_low_ref, to_high_ref,
):
    queries = q_ref.shape[0]
    rim = low_ref.shape[1]
    keys = queries + 2 * rim
    allowed = window_mask(first_ref[0], total_rows, breadth, keys, queries)
    heads = range(q_ref.shape[1] // HEAD_DIM)
    scores = [
        dot(window_of(k_ref, low_ref, high_ref, 0, head), q_ref[:, lanes(head)], NT) for head in heads
    ]
    grads = [head_rows(g_ref, head) for head in heads]
    prob_grads = [
        dot(window_of(v_ref, low_ref, high_ref, 1, head), grads[head], NT) for head in heads
    ]
    weights, score_grads = [], []
    for head in heads:
        probs = softmax_columns(jnp.where(allowed, scores[head], NEG_FILL))
        weights.append(probs.astype(BF16))
        grad_dot = jnp.sum(weights[head].astype(F32) * prob_grads[head], 0, keepdims=True)
        score_grads.append((probs * (prob_grads[head] - grad_dot)).astype(BF16))
    values = [dot(weights[head], grads[head], NN) for head in heads]
    keys = [dot(score_grads[head], q_ref[:, lanes(head)], NN) * SCALING for head in heads]
    for wide, own_ref, half in (
        (keys, ks_ref, 0),
        (values, vs_ref, 1),
    ):
        for head in heads:
            at = lanes(head)
            own_ref[:, at] = wide[head][rim : rim + queries]
            to_low_ref[half, :, at] = wide[head][:rim].astype(BF16)
            to_high_ref[half, :, at] = wide[head][rim + queries :].astype(BF16)
    for head in heads:
        key = window_of(k_ref, low_ref, high_ref, 0, head)
        query_sum = dot(score_grads[head], key, TN) * SCALING
        qs_ref[:, :, lanes(head)] = chunked(query_sum, qs_ref.shape[0]).astype(BF16)


def same_position(rows, spots):
    left = lax.broadcasted_iota(jnp.int32, (rows, rows), 0)
    right = lax.broadcasted_iota(jnp.int32, (rows, rows), 1)
    return left % spots == right % spots


def temporal_scores_kernel(moved_ref, begun_ref, sent_ref, probs_ref, held, sems):
    del begun_ref
    frames, spots = moved_ref.shape[0], moved_ref.shape[1]
    channels = HEADS * HEAD_DIM
    same = same_position(frames * spots, spots)
    stores = []
    for group in range(HEADS // TIME_HEADS):
        heads = range(group * TIME_HEADS, (group + 1) * TIME_HEADS)
        scores = [
            dot(head_rows(moved_ref, HEADS + head), head_rows(moved_ref, head), NT) for head in heads
        ]
        probs = [softmax_columns(jnp.where(same, part, NEG_FILL)) for part in scores]
        grads = [
            dot(part.astype(BF16), head_rows(moved_ref, 2 * HEADS + head), NN)
            for part, head in zip(probs, heads)
        ]
        for part, head in zip(probs, heads):
            probs_ref[head] = part
        for part, head in zip(grads, heads):
            held[:, :, lanes(head)] = chunked(part, frames).astype(BF16)
        first, last = group * TIME_HEADS * HEAD_DIM, (group + 1) * TIME_HEADS * HEAD_DIM
        stores.append(
            started(
                held.at[:, :, first:last],
                sent_ref.at[:, :, channels + first : channels + last],
                sems.at[group],
            )
        )
    for store in stores:
        store.wait()


def temporal_grads_kernel(moved_ref, both_ref, probs_ref, out_ref, grad_ref, held, sems):
    frames = moved_ref.shape[0]
    width = TIME_HEADS * HEAD_DIM
    groups = range(HEADS // TIME_HEADS)
    stores = [started(both_ref.at[:, :, HEADS * HEAD_DIM :], grad_ref, sems.at[3 * len(groups)])]
    for group in groups:
        heads = range(group * TIME_HEADS, (group + 1) * TIME_HEADS)
        spatial = [head_rows(both_ref, head) for head in heads]
        prob_grads = [
            dot(part, head_rows(moved_ref, 2 * HEADS + head), NT) for part, head in zip(spatial, heads)
        ]
        outs = [dot(probs_ref[head].astype(BF16), part, TN) for part, head in zip(spatial, heads)]
        score_grads = []
        for prob_grad, head in zip(prob_grads, heads):
            probs = probs_ref[head]
            weights = probs.astype(BF16).astype(F32)
            grad_dot = jnp.sum(weights * prob_grad, 0, keepdims=True)
            score_grads.append((probs * (prob_grad - grad_dot)).astype(BF16))
        query_parts = [
            dot(part, head_rows(moved_ref, HEADS + head), TN) * SCALING
            for part, head in zip(score_grads, heads)
        ]
        key_parts = [
            dot(part, head_rows(moved_ref, head), NN) * SCALING for part, head in zip(score_grads, heads)
        ]
        for place, parts in enumerate((outs, query_parts, key_parts)):
            piece = group * 3 + place
            for step, part in enumerate(parts):
                first = piece * width + step * HEAD_DIM
                held[:, :, first : first + HEAD_DIM] = chunked(part, frames).astype(BF16)
            at = slice(piece * width, (piece + 1) * width)
            stores.append(started(held.at[:, :, at], out_ref.at[:, :, at], sems.at[piece]))
    for store in stores:
        store.wait()


def rims_kernel(k_first_ref, v_first_ref, k_last_ref, v_last_ref, to_low_ref, to_high_ref):
    to_low_ref[0] = k_first_ref[...]
    to_low_ref[1] = v_first_ref[...]
    to_high_ref[0] = k_last_ref[...]
    to_high_ref[1] = v_last_ref[...]


def started(source, target, sem):
    copy = pltpu.make_async_copy(source, target, sem)
    copy.start()
    return copy


def join_kernel(*refs):
    sources, (joined_ref, held, load_sems, store_sems) = refs[:-4], refs[-4:]
    pieces = load_sems.shape[0]
    chunks, width = joined_ref.shape[0] // pieces, sources[0].shape[2]
    loads = []
    for piece in range(pieces):
        rows = slice(piece * chunks, (piece + 1) * chunks)
        loads.append(
            [
                started(
                    source.at[rows],
                    held.at[rows, :, place * width : (place + 1) * width],
                    load_sems.at[piece, place],
                )
                for place, source in enumerate(sources)
            ]
        )
    stores = []
    for piece in range(pieces):
        rows = slice(piece * chunks, (piece + 1) * chunks)
        for load in loads[piece]:
            load.wait()
        stores.append(started(held.at[rows], joined_ref.at[rows], store_sems.at[piece]))
    for store in stores:
        store.wait()


def rim_add_kernel(ks_ref, vs_ref, from_low_ref, from_high_ref, key_ref, value_ref):
    rim = from_low_ref.shape[1]
    rows = ks_ref.shape[0]
    totals = [
        jnp.concatenate(
            [
                sum_ref[:rim] + from_low_ref[half].astype(F32),
                sum_ref[rim : rows - rim],
                sum_ref[rows - rim :] + from_high_ref[half].astype(F32),
            ],
            0,
        )
        for half, sum_ref in enumerate((ks_ref, vs_ref))
    ]
    key_ref[...] = chunked(totals[0], key_ref.shape[0]).astype(BF16)
    value_ref[...] = totals[1].astype(BF16)


def last_sum_kernel(back_ref, qs_ref, ks_ref, *refs):
    outs, (back, qs, ks), results, (load_sems, store_sems) = refs[:3], refs[3:6], refs[6:8], refs[8:]
    pieces = load_sems.shape[0]
    chunks = back.shape[0] // pieces
    width = TIME_HEADS * HEAD_DIM
    groups = range(HEADS // TIME_HEADS)
    pairs = ((back_ref, back), (qs_ref, qs), (ks_ref, ks))
    somes = [slice(piece * chunks, (piece + 1) * chunks) for piece in range(pieces)]
    loads, stores = [], []
    for piece, some in enumerate(somes):
        loads.append(
            [
                started(source.at[some], target.at[some], load_sems.at[piece, place])
                for place, (source, target) in enumerate(pairs)
            ]
        )
    for piece, some in enumerate(somes):
        for load in loads[piece]:
            load.wait()
        for group in groups:
            to = slice(group * width, (group + 1) * width)
            first = group * 3 * width
            stores.append(
                started(
                    back.at[some, :, first : first + width],
                    outs[0].at[some, :, to],
                    store_sems.at[piece, group],
                )
            )
            for place, (kept, result) in enumerate(((qs, results[0]), (ks, results[1]))):
                first += width
                part = back[some, :, first : first + width].astype(F32)
                result[some, :, to] = (part + kept[some, :, to].astype(F32)).astype(BF16)
        for place in range(2):
            stores.append(
                started(
                    results[place].at[some],
                    outs[1 + place].at[some],
                    store_sems.at[piece, len(groups) + place],
                )
            )
    for store in stores:
        store.wait()


def in_hbm(tensor):
    return pltpu.with_memory_space_constraint(tensor, pltpu.HBM)


def in_vmem(tensor):
    return pltpu.with_memory_space_constraint(tensor, pltpu.VMEM)


def exchange(chunks):
    return lax.all_to_all(chunks, "tm", split_axis=0, concat_axis=0, tiled=True)


def on_device(queries, key_states, value_states, out_grad):
    band_rows, breadth, channels = queries.shape[1:]
    tokens = band_rows * breadth
    rim = RADIUS * breadth
    parts = lax.axis_size("tm")
    bands = lax.axis_size("rows")
    spots = tokens // parts
    band = lax.axis_index("rows").astype(jnp.int32)
    first_row = (band * band_rows).reshape(1)
    total_rows = bands * band_rows
    upward = [(i, i + 1) for i in range(bands - 1)]
    downward = [(i + 1, i) for i in range(bands - 1)]

    scalar = pl.BlockSpec(memory_space=pltpu.SMEM)
    anywhere = pl.BlockSpec(memory_space=pl.ANY)

    def rows_block(rows, heads):
        return pl.BlockSpec((rows, heads * HEAD_DIM), lambda i: (0, i))

    def rims_block(heads):
        return pl.BlockSpec((2, rim, heads * HEAD_DIM), lambda i: (0, 0, i))

    def chunk_block(heads, offset, stride=1):
        return pl.BlockSpec((parts, spots, heads * HEAD_DIM), lambda i: (0, 0, i * stride + offset))

    query, key, value = (
        tensor.reshape(tokens, channels) for tensor in (queries, key_states, value_states)
    )
    rims = jax.ShapeDtypeStruct((2, rim, channels), BF16)
    first_rows = pl.BlockSpec((breadth, channels), lambda i: (i, 0))
    last_rows = pl.BlockSpec((breadth, channels), lambda i: (i + band_rows - RADIUS, 0))
    rim_rows = pl.BlockSpec((2, breadth, channels), lambda i: (0, i, 0))
    to_low, to_high = call(
        rims_kernel,
        RADIUS,
        [first_rows, first_rows, last_rows, last_rows],
        [rim_rows, rim_rows],
        [pltpu.HBM(rims.shape, BF16)] * 2,
    )(*map(in_hbm, (key, value, key, value)))
    low = lax.ppermute(to_high, "rows", upward)
    high = lax.ppermute(to_low, "rows", downward)

    joined_shape = (parts, spots, 3 * channels)
    joined = pl.pallas_call(
        join_kernel,
        in_specs=[anywhere] * 3,
        out_specs=anywhere,
        out_shape=pltpu.HBM(joined_shape, BF16),
        scratch_shapes=[
            pltpu.VMEM(joined_shape, BF16),
            pltpu.SemaphoreType.DMA((PIECES, 3)),
            pltpu.SemaphoreType.DMA((PIECES,)),
        ],
        compiler_params=params,
    )(*(in_hbm(tensor.reshape(parts, spots, channels)) for tensor in (queries, key_states, out_grad)))
    moved = exchange(joined)

    own = rows_block(tokens, FWD_HEADS)
    sent = call(
        functools.partial(spatial_fwd_kernel, total_rows, breadth),
        HEADS // FWD_HEADS,
        [scalar, own, own, own, rims_block(FWD_HEADS), rims_block(FWD_HEADS)],
        chunk_block(FWD_HEADS, 0),
        pltpu.HBM((parts, spots, 2 * channels), BF16),
    )(first_row, query, key, value, low, high)

    moved = in_vmem(moved)
    groups = HEADS // TIME_HEADS
    in_place = pl.BlockSpec(memory_space=pltpu.VMEM)
    sent, probs = pl.pallas_call(
        temporal_scores_kernel,
        in_specs=[in_place, anywhere],
        out_specs=[anywhere, in_place],
        out_shape=[pltpu.HBM(sent.shape, BF16), pltpu.VMEM((HEADS, tokens, tokens), F32)],
        scratch_shapes=[
            pltpu.VMEM((parts, spots, channels), BF16),
            pltpu.SemaphoreType.DMA((groups,)),
        ],
        input_output_aliases={1: 0},
        compiler_params=params,
    )(moved, in_hbm(sent))
    both = in_vmem(exchange(sent))

    parts_out, spatial_grad = pl.pallas_call(
        temporal_grads_kernel,
        in_specs=[in_place] * 3,
        out_specs=[anywhere] * 2,
        out_shape=[pltpu.HBM(joined_shape, BF16), pltpu.HBM((parts, spots, channels), BF16)],
        scratch_shapes=[pltpu.VMEM(joined_shape, BF16), pltpu.SemaphoreType.DMA((3 * groups + 1,))],
        compiler_params=params,
    )(moved, both, in_vmem(probs))
    back = exchange(parts_out)

    count = HEADS // BWD_HEADS
    own = rows_block(tokens, BWD_HEADS)
    whole = jax.ShapeDtypeStruct((tokens, channels), F32)
    qs, ks, vs, to_low, to_high = call(
        functools.partial(spatial_bwd_kernel, total_rows, breadth),
        count,
        [scalar, own, own, own, rims_block(BWD_HEADS), rims_block(BWD_HEADS), chunk_block(BWD_HEADS, 0)],
        [chunk_block(BWD_HEADS, 0), own, own, rims_block(BWD_HEADS), rims_block(BWD_HEADS)],
        [pltpu.HBM((parts, spots, channels), BF16), whole, whole, rims, rims],
    )(first_row, query, key, value, low, high, in_hbm(spatial_grad))
    from_high = lax.ppermute(to_low, "rows", downward)
    from_low = lax.ppermute(to_high, "rows", upward)
    final = jax.ShapeDtypeStruct((tokens, channels), BF16)
    own = rows_block(tokens, RIM_HEADS)
    ks, value_grad = call(
        rim_add_kernel,
        HEADS // RIM_HEADS,
        [own, own, rims_block(RIM_HEADS), rims_block(RIM_HEADS)],
        [chunk_block(RIM_HEADS, 0), own],
        [pltpu.HBM((parts, spots, channels), BF16), final],
    )(ks, vs, from_low, from_high)

    temporal_out, query_grad, key_grad = pl.pallas_call(
        last_sum_kernel,
        in_specs=[anywhere] * 3,
        out_specs=[anywhere] * 3,
        out_shape=[pltpu.HBM((parts, spots, channels), BF16)] * 3,
        scratch_shapes=[pltpu.VMEM(joined_shape, BF16)]
        + [pltpu.VMEM((parts, spots, channels), BF16)] * 4
        + [pltpu.SemaphoreType.DMA((PIECES, 3)), pltpu.SemaphoreType.DMA((PIECES, groups + 2))],
        compiler_params=params,
    )(back, in_hbm(qs), in_hbm(ks))
    return tuple(
        tensor.reshape(queries.shape) for tensor in (temporal_out, query_grad, key_grad, value_grad)
    )


def solution(mesh):
    placed = P("tm", "rows", None, None)
    return jax.shard_map(
        on_device,
        mesh=mesh,
        in_specs=(placed,) * 4,
        out_specs=(placed,) * 4,
        check_vma=False,
    )
```

```python
import functools

import jax
import jax.numpy as jnp
from jax import lax
from jax.experimental import pallas as pl
from jax.experimental.pallas import tpu as pltpu
from jax.sharding import PartitionSpec as P

HEADS = 24
HEAD_DIM = 128
RADIUS = 3
SCALING = HEAD_DIM ** (-0.5)
NEG_FILL = -1e30
BF16 = jnp.bfloat16
F32 = jnp.float32

FWD_HEADS = 4
TIME_HEADS = 12
BWD_HEADS = 4
RIM_HEADS = 8
PIECES = 4

NT = (((1,), (1,)), ((), ()))
NN = (((1,), (0,)), ((), ()))
TN = (((0,), (0,)), ((), ()))


def dot(left, right, dims):
    return lax.dot_general(left, right, dims, preferred_element_type=F32)


def lanes(head):
    return slice(head * HEAD_DIM, (head + 1) * HEAD_DIM)


def flat_rows(chunks):
    wide = chunks.astype(F32)
    return wide.reshape(wide.shape[0] * wide.shape[1], wide.shape[2])


def head_rows(ref, head):
    return flat_rows(ref[:, :, lanes(head)]).astype(BF16)


def chunked(matrix, chunks):
    return matrix.reshape(chunks, matrix.shape[0] // chunks, matrix.shape[1])


def softmax_columns(scores):
    peak = jnp.max(scores, 0, keepdims=True)
    grown = jnp.exp((scores - peak) * SCALING)
    return grown * (1.0 / jnp.sum(grown, 0, keepdims=True))


params = pltpu.CompilerParams(vmem_limit_bytes=16 * 1024 * 1024)


def call(kernel, grid, in_specs, out_specs, out_shape, **more):
    return pl.pallas_call(
        kernel,
        grid=(grid,),
        in_specs=in_specs,
        out_specs=out_specs,
        out_shape=out_shape,
        compiler_params=params,
        **more,
    )


def window_mask(first_row, total_rows, breadth, keys, queries, reach=RADIUS):
    key = lax.broadcasted_iota(jnp.int32, (keys, queries), 0)
    query = lax.broadcasted_iota(jnp.int32, (keys, queries), 1)
    row_step = key // breadth - reach - query // breadth
    col_step = key % breadth - query % breadth
    key_row = first_row - reach + key // breadth
    return (
        (jnp.abs(row_step) <= RADIUS)
        & (jnp.abs(col_step) <= RADIUS)
        & (key_row >= 0)
        & (key_row < total_rows)
    )


def window_of(own_ref, low_ref, high_ref, half, head):
    at = lanes(head)
    return jnp.concatenate([low_ref[half, :, at], own_ref[:, at], high_ref[half, :, at]], 0)


def spatial_fwd_kernel(total_rows, breadth, first_ref, q_ref, k_ref, v_ref, low_ref, high_ref, s_ref):
    queries = q_ref.shape[0]
    keys = queries + 2 * low_ref.shape[1]
    allowed = window_mask(first_ref[0], total_rows, breadth, keys, queries)
    heads = range(q_ref.shape[1] // HEAD_DIM)
    scores = [
        dot(window_of(k_ref, low_ref, high_ref, 0, head), q_ref[:, lanes(head)], NT) for head in heads
    ]
    weights = [softmax_columns(jnp.where(allowed, part, NEG_FILL)).astype(BF16) for part in scores]
    outs = [dot(weights[head], window_of(v_ref, low_ref, high_ref, 1, head), TN) for head in heads]
    for head in heads:
        s_ref[:, :, lanes(head)] = chunked(outs[head], s_ref.shape[0]).astype(BF16)


def spatial_bwd_kernel(
    total_rows, breadth, first_ref, q_ref, k_ref, v_ref, low_ref, high_ref, g_ref,
    qs_ref, ks_ref, vs_ref, to_low_ref, to_high_ref,
):
    queries = q_ref.shape[0]
    rim = low_ref.shape[1]
    keys = queries + 2 * rim
    allowed = window_mask(first_ref[0], total_rows, breadth, keys, queries)
    heads = range(q_ref.shape[1] // HEAD_DIM)
    scores = [
        dot(window_of(k_ref, low_ref, high_ref, 0, head), q_ref[:, lanes(head)], NT) for head in heads
    ]
    grads = [head_rows(g_ref, head) for head in heads]
    prob_grads = [
        dot(window_of(v_ref, low_ref, high_ref, 1, head), grads[head], NT) for head in heads
    ]
    weights, score_grads = [], []
    for head in heads:
        probs = softmax_columns(jnp.where(allowed, scores[head], NEG_FILL))
        weights.append(probs.astype(BF16))
        grad_dot = jnp.sum(weights[head].astype(F32) * prob_grads[head], 0, keepdims=True)
        score_grads.append((probs * (prob_grads[head] - grad_dot)).astype(BF16))
    values = [dot(weights[head], grads[head], NN) for head in heads]
    keys = [dot(score_grads[head], q_ref[:, lanes(head)], NN) * SCALING for head in heads]
    for wide, own_ref, half in (
        (keys, ks_ref, 0),
        (values, vs_ref, 1),
    ):
        for head in heads:
            at = lanes(head)
            own_ref[:, at] = wide[head][rim : rim + queries]
            to_low_ref[half, :, at] = wide[head][:rim].astype(BF16)
            to_high_ref[half, :, at] = wide[head][rim + queries :].astype(BF16)
    for head in heads:
        key = window_of(k_ref, low_ref, high_ref, 0, head)
        query_sum = dot(score_grads[head], key, TN) * SCALING
        qs_ref[:, :, lanes(head)] = chunked(query_sum, qs_ref.shape[0]).astype(BF16)


def same_position(rows, spots):
    left = lax.broadcasted_iota(jnp.int32, (rows, rows), 0)
    right = lax.broadcasted_iota(jnp.int32, (rows, rows), 1)
    return left % spots == right % spots


def temporal_scores_kernel(moved_ref, begun_ref, sent_ref, probs_ref, held, sems):
    del begun_ref
    frames, spots = moved_ref.shape[0], moved_ref.shape[1]
    channels = HEADS * HEAD_DIM
    same = same_position(frames * spots, spots)
    stores = []
    for group in range(HEADS // TIME_HEADS):
        heads = range(group * TIME_HEADS, (group + 1) * TIME_HEADS)
        scores = [
            dot(head_rows(moved_ref, HEADS + head), head_rows(moved_ref, head), NT) for head in heads
        ]
        probs = [softmax_columns(jnp.where(same, part, NEG_FILL)) for part in scores]
        grads = [
            dot(part.astype(BF16), head_rows(moved_ref, 2 * HEADS + head), NN)
            for part, head in zip(probs, heads)
        ]
        for part, head in zip(probs, heads):
            probs_ref[head] = part
        for part, head in zip(grads, heads):
            held[:, :, lanes(head)] = chunked(part, frames).astype(BF16)
        first, last = group * TIME_HEADS * HEAD_DIM, (group + 1) * TIME_HEADS * HEAD_DIM
        stores.append(
            started(
                held.at[:, :, first:last],
                sent_ref.at[:, :, channels + first : channels + last],
                sems.at[group],
            )
        )
    for store in stores:
        store.wait()


def temporal_grads_kernel(moved_ref, both_ref, probs_ref, out_ref, grad_ref, held, sems):
    frames = moved_ref.shape[0]
    width = TIME_HEADS * HEAD_DIM
    groups = range(HEADS // TIME_HEADS)
    stores = [started(both_ref.at[:, :, HEADS * HEAD_DIM :], grad_ref, sems.at[3 * len(groups)])]
    for group in groups:
        heads = range(group * TIME_HEADS, (group + 1) * TIME_HEADS)
        spatial = [head_rows(both_ref, head) for head in heads]
        prob_grads = [
            dot(part, head_rows(moved_ref, 2 * HEADS + head), NT) for part, head in zip(spatial, heads)
        ]
        outs = [dot(probs_ref[head].astype(BF16), part, TN) for part, head in zip(spatial, heads)]
        score_grads = []
        for prob_grad, head in zip(prob_grads, heads):
            probs = probs_ref[head]
            weights = probs.astype(BF16).astype(F32)
            grad_dot = jnp.sum(weights * prob_grad, 0, keepdims=True)
            score_grads.append((probs * (prob_grad - grad_dot)).astype(BF16))
        query_parts = [
            dot(part, head_rows(moved_ref, HEADS + head), TN) * SCALING
            for part, head in zip(score_grads, heads)
        ]
        key_parts = [
            dot(part, head_rows(moved_ref, head), NN) * SCALING for part, head in zip(score_grads, heads)
        ]
        for place, parts in enumerate((outs, query_parts, key_parts)):
            piece = group * 3 + place
            for step, part in enumerate(parts):
                first = piece * width + step * HEAD_DIM
                held[:, :, first : first + HEAD_DIM] = chunked(part, frames).astype(BF16)
            at = slice(piece * width, (piece + 1) * width)
            stores.append(started(held.at[:, :, at], out_ref.at[:, :, at], sems.at[piece]))
    for store in stores:
        store.wait()


def rims_kernel(k_first_ref, v_first_ref, k_last_ref, v_last_ref, to_low_ref, to_high_ref):
    to_low_ref[0] = k_first_ref[...]
    to_low_ref[1] = v_first_ref[...]
    to_high_ref[0] = k_last_ref[...]
    to_high_ref[1] = v_last_ref[...]


def started(source, target, sem):
    copy = pltpu.make_async_copy(source, target, sem)
    copy.start()
    return copy


def join_kernel(*refs):
    sources, (joined_ref, held, load_sems, store_sems) = refs[:-4], refs[-4:]
    pieces = load_sems.shape[0]
    chunks, width = joined_ref.shape[0] // pieces, sources[0].shape[2]
    loads = []
    for piece in range(pieces):
        rows = slice(piece * chunks, (piece + 1) * chunks)
        loads.append(
            [
                started(
                    source.at[rows],
                    held.at[rows, :, place * width : (place + 1) * width],
                    load_sems.at[piece, place],
                )
                for place, source in enumerate(sources)
            ]
        )
    stores = []
    for piece in range(pieces):
        rows = slice(piece * chunks, (piece + 1) * chunks)
        for load in loads[piece]:
            load.wait()
        stores.append(started(held.at[rows], joined_ref.at[rows], store_sems.at[piece]))
    for store in stores:
        store.wait()


def rim_add_kernel(ks_ref, vs_ref, from_low_ref, from_high_ref, key_ref, value_ref):
    rim = from_low_ref.shape[1]
    rows = ks_ref.shape[0]
    totals = [
        jnp.concatenate(
            [
                sum_ref[:rim] + from_low_ref[half].astype(F32),
                sum_ref[rim : rows - rim],
                sum_ref[rows - rim :] + from_high_ref[half].astype(F32),
            ],
            0,
        )
        for half, sum_ref in enumerate((ks_ref, vs_ref))
    ]
    key_ref[...] = chunked(totals[0], key_ref.shape[0]).astype(BF16)
    value_ref[...] = totals[1].astype(BF16)


def last_sum_kernel(back_ref, qs_ref, ks_ref, *refs):
    outs, (back, qs, ks), results, (load_sems, store_sems) = refs[:3], refs[3:6], refs[6:8], refs[8:]
    pieces = load_sems.shape[0]
    chunks = back.shape[0] // pieces
    width = TIME_HEADS * HEAD_DIM
    groups = range(HEADS // TIME_HEADS)
    pairs = ((back_ref, back), (qs_ref, qs), (ks_ref, ks))
    somes = [slice(piece * chunks, (piece + 1) * chunks) for piece in range(pieces)]
    loads, stores = [], []
    for piece, some in enumerate(somes):
        loads.append(
            [
                started(source.at[some], target.at[some], load_sems.at[piece, place])
                for place, (source, target) in enumerate(pairs)
            ]
        )
    for piece, some in enumerate(somes):
        for load in loads[piece]:
            load.wait()
        for group in groups:
            to = slice(group * width, (group + 1) * width)
            first = group * 3 * width
            stores.append(
                started(
                    back.at[some, :, first : first + width],
                    outs[0].at[some, :, to],
                    store_sems.at[piece, group],
                )
            )
            for place, (kept, result) in enumerate(((qs, results[0]), (ks, results[1]))):
                first += width
                part = back[some, :, first : first + width].astype(F32)
                result[some, :, to] = (part + kept[some, :, to].astype(F32)).astype(BF16)
        for place in range(2):
            stores.append(
                started(
                    results[place].at[some],
                    outs[1 + place].at[some],
                    store_sems.at[piece, len(groups) + place],
                )
            )
    for store in stores:
        store.wait()


def in_hbm(tensor):
    return pltpu.with_memory_space_constraint(tensor, pltpu.HBM)


def in_vmem(tensor):
    return pltpu.with_memory_space_constraint(tensor, pltpu.VMEM)


def exchange(chunks):
    return lax.all_to_all(chunks, "tm", split_axis=0, concat_axis=0, tiled=True)


def on_device(queries, key_states, value_states, out_grad):
    band_rows, breadth, channels = queries.shape[1:]
    tokens = band_rows * breadth
    rim = RADIUS * breadth
    parts = lax.axis_size("tm")
    bands = lax.axis_size("rows")
    spots = tokens // parts
    band = lax.axis_index("rows").astype(jnp.int32)
    first_row = (band * band_rows).reshape(1)
    total_rows = bands * band_rows
    upward = [(i, i + 1) for i in range(bands - 1)]
    downward = [(i + 1, i) for i in range(bands - 1)]

    scalar = pl.BlockSpec(memory_space=pltpu.SMEM)
    anywhere = pl.BlockSpec(memory_space=pl.ANY)

    def rows_block(rows, heads):
        return pl.BlockSpec((rows, heads * HEAD_DIM), lambda i: (0, i))

    def rims_block(heads):
        return pl.BlockSpec((2, rim, heads * HEAD_DIM), lambda i: (0, 0, i))

    def chunk_block(heads, offset, stride=1):
        return pl.BlockSpec((parts, spots, heads * HEAD_DIM), lambda i: (0, 0, i * stride + offset))

    query, key, value = (
        tensor.reshape(tokens, channels) for tensor in (queries, key_states, value_states)
    )
    rims = jax.ShapeDtypeStruct((2, rim, channels), BF16)
    first_rows = pl.BlockSpec((breadth, channels), lambda i: (i, 0))
    last_rows = pl.BlockSpec((breadth, channels), lambda i: (i + band_rows - RADIUS, 0))
    rim_rows = pl.BlockSpec((2, breadth, channels), lambda i: (0, i, 0))
    to_low, to_high = call(
        rims_kernel,
        RADIUS,
        [first_rows, first_rows, last_rows, last_rows],
        [rim_rows, rim_rows],
        [pltpu.HBM(rims.shape, BF16)] * 2,
    )(*map(in_hbm, (key, value, key, value)))
    low = lax.ppermute(to_high, "rows", upward)
    high = lax.ppermute(to_low, "rows", downward)

    joined_shape = (parts, spots, 3 * channels)
    joined = pl.pallas_call(
        join_kernel,
        in_specs=[anywhere] * 3,
        out_specs=anywhere,
        out_shape=pltpu.HBM(joined_shape, BF16),
        scratch_shapes=[
            pltpu.VMEM(joined_shape, BF16),
            pltpu.SemaphoreType.DMA((PIECES, 3)),
            pltpu.SemaphoreType.DMA((PIECES,)),
        ],
        compiler_params=params,
    )(*(in_hbm(tensor.reshape(parts, spots, channels)) for tensor in (queries, key_states, out_grad)))
    moved = exchange(joined)

    own = rows_block(tokens, FWD_HEADS)
    sent = call(
        functools.partial(spatial_fwd_kernel, total_rows, breadth),
        HEADS // FWD_HEADS,
        [scalar, own, own, own, rims_block(FWD_HEADS), rims_block(FWD_HEADS)],
        chunk_block(FWD_HEADS, 0),
        pltpu.HBM((parts, spots, 2 * channels), BF16),
    )(first_row, query, key, value, low, high)

    moved = in_vmem(moved)
    groups = HEADS // TIME_HEADS
    in_place = pl.BlockSpec(memory_space=pltpu.VMEM)
    sent, probs = pl.pallas_call(
        temporal_scores_kernel,
        in_specs=[in_place, anywhere],
        out_specs=[anywhere, in_place],
        out_shape=[pltpu.HBM(sent.shape, BF16), pltpu.VMEM((HEADS, tokens, tokens), F32)],
        scratch_shapes=[
            pltpu.VMEM((parts, spots, channels), BF16),
            pltpu.SemaphoreType.DMA((groups,)),
        ],
        input_output_aliases={1: 0},
        compiler_params=params,
    )(moved, in_hbm(sent))
    both = in_vmem(exchange(sent))

    parts_out, spatial_grad = pl.pallas_call(
        temporal_grads_kernel,
        in_specs=[in_place] * 3,
        out_specs=[anywhere] * 2,
        out_shape=[pltpu.HBM(joined_shape, BF16), pltpu.HBM((parts, spots, channels), BF16)],
        scratch_shapes=[pltpu.VMEM(joined_shape, BF16), pltpu.SemaphoreType.DMA((3 * groups + 1,))],
        compiler_params=params,
    )(moved, both, in_vmem(probs))
    back = exchange(parts_out)

    count = HEADS // BWD_HEADS
    own = rows_block(tokens, BWD_HEADS)
    whole = jax.ShapeDtypeStruct((tokens, channels), F32)
    qs, ks, vs, to_low, to_high = call(
        functools.partial(spatial_bwd_kernel, total_rows, breadth),
        count,
        [scalar, own, own, own, rims_block(BWD_HEADS), rims_block(BWD_HEADS), chunk_block(BWD_HEADS, 0)],
        [chunk_block(BWD_HEADS, 0), own, own, rims_block(BWD_HEADS), rims_block(BWD_HEADS)],
        [pltpu.HBM((parts, spots, channels), BF16), whole, whole, rims, rims],
    )(first_row, query, key, value, low, high, in_hbm(spatial_grad))
    from_high = lax.ppermute(to_low, "rows", downward)
    from_low = lax.ppermute(to_high, "rows", upward)
    final = jax.ShapeDtypeStruct((tokens, channels), BF16)
    own = rows_block(tokens, RIM_HEADS)
    ks, value_grad = call(
        rim_add_kernel,
        HEADS // RIM_HEADS,
        [own, own, rims_block(RIM_HEADS), rims_block(RIM_HEADS)],
        [chunk_block(RIM_HEADS, 0), own],
        [pltpu.HBM((parts, spots, channels), BF16), final],
    )(ks, vs, from_low, from_high)

    temporal_out, query_grad, key_grad = pl.pallas_call(
        last_sum_kernel,
        in_specs=[anywhere] * 3,
        out_specs=[anywhere] * 3,
        out_shape=[pltpu.HBM((parts, spots, channels), BF16)] * 3,
        scratch_shapes=[pltpu.VMEM(joined_shape, BF16)]
        + [pltpu.VMEM((parts, spots, channels), BF16)] * 4
        + [pltpu.SemaphoreType.DMA((PIECES, 3)), pltpu.SemaphoreType.DMA((PIECES, groups + 2))],
        compiler_params=params,
    )(back, in_hbm(qs), in_hbm(ks))
    return tuple(
        tensor.reshape(queries.shape) for tensor in (temporal_out, query_grad, key_grad, value_grad)
    )


def solution(mesh):
    placed = P("tm", "rows", None, None)
    return jax.shard_map(
        on_device,
        mesh=mesh,
        in_specs=(placed,) * 4,
        out_specs=(placed,) * 4,
        check_vma=False,
    )
```

```python
import functools

import jax
import jax.numpy as jnp
from jax import lax
from jax.experimental import pallas as pl
from jax.experimental.pallas import tpu as pltpu
from jax.sharding import PartitionSpec as P

HEADS = 24
HEAD_DIM = 128
RADIUS = 3
SCALING = HEAD_DIM ** (-0.5)
NEG_FILL = -1e30
BF16 = jnp.bfloat16
F32 = jnp.float32

FWD_HEADS = 4
TIME_HEADS = 12
BWD_HEADS = 4
RIM_HEADS = 8
PIECES = 4

NT = (((1,), (1,)), ((), ()))
NN = (((1,), (0,)), ((), ()))
TN = (((0,), (0,)), ((), ()))


def dot(left, right, dims):
    return lax.dot_general(left, right, dims, preferred_element_type=F32)


def lanes(head):
    return slice(head * HEAD_DIM, (head + 1) * HEAD_DIM)


def flat_rows(chunks):
    wide = chunks.astype(F32)
    return wide.reshape(wide.shape[0] * wide.shape[1], wide.shape[2])


def head_rows(ref, head):
    return flat_rows(ref[:, :, lanes(head)]).astype(BF16)


def chunked(matrix, chunks):
    return matrix.reshape(chunks, matrix.shape[0] // chunks, matrix.shape[1])


def softmax_columns(scores):
    peak = jnp.max(scores, 0, keepdims=True)
    grown = jnp.exp((scores - peak) * SCALING)
    return grown * (1.0 / jnp.sum(grown, 0, keepdims=True))


params = pltpu.CompilerParams(vmem_limit_bytes=16 * 1024 * 1024)


def call(kernel, grid, in_specs, out_specs, out_shape, **more):
    return pl.pallas_call(
        kernel,
        grid=(grid,),
        in_specs=in_specs,
        out_specs=out_specs,
        out_shape=out_shape,
        compiler_params=params,
        **more,
    )


def window_mask(first_row, total_rows, breadth, keys, queries, reach=RADIUS):
    key = lax.broadcasted_iota(jnp.int32, (keys, queries), 0)
    query = lax.broadcasted_iota(jnp.int32, (keys, queries), 1)
    row_step = key // breadth - reach - query // breadth
    col_step = key % breadth - query % breadth
    key_row = first_row - reach + key // breadth
    return (
        (jnp.abs(row_step) <= RADIUS)
        & (jnp.abs(col_step) <= RADIUS)
        & (key_row >= 0)
        & (key_row < total_rows)
    )


def window_of(own_ref, low_ref, high_ref, half, head):
    at = lanes(head)
    return jnp.concatenate([low_ref[half, :, at], own_ref[:, at], high_ref[half, :, at]], 0)


def spatial_fwd_kernel(total_rows, breadth, first_ref, q_ref, k_ref, v_ref, low_ref, high_ref, s_ref):
    queries = q_ref.shape[0]
    keys = queries + 2 * low_ref.shape[1]
    allowed = window_mask(first_ref[0], total_rows, breadth, keys, queries)
    heads = range(q_ref.shape[1] // HEAD_DIM)
    scores = [
        dot(window_of(k_ref, low_ref, high_ref, 0, head), q_ref[:, lanes(head)], NT) for head in heads
    ]
    weights = [softmax_columns(jnp.where(allowed, part, NEG_FILL)).astype(BF16) for part in scores]
    outs = [dot(weights[head], window_of(v_ref, low_ref, high_ref, 1, head), TN) for head in heads]
    for head in heads:
        s_ref[:, :, lanes(head)] = chunked(outs[head], s_ref.shape[0]).astype(BF16)


def spatial_bwd_kernel(
    total_rows, breadth, first_ref, q_ref, k_ref, v_ref, low_ref, high_ref, g_ref,
    qs_ref, ks_ref, vs_ref, to_low_ref, to_high_ref,
):
    queries = q_ref.shape[0]
    rim = low_ref.shape[1]
    keys = queries + 2 * rim
    allowed = window_mask(first_ref[0], total_rows, breadth, keys, queries)
    heads = range(q_ref.shape[1] // HEAD_DIM)
    scores = [
        dot(window_of(k_ref, low_ref, high_ref, 0, head), q_ref[:, lanes(head)], NT) for head in heads
    ]
    grads = [head_rows(g_ref, head) for head in heads]
    prob_grads = [
        dot(window_of(v_ref, low_ref, high_ref, 1, head), grads[head], NT) for head in heads
    ]
    weights, score_grads = [], []
    for head in heads:
        probs = softmax_columns(jnp.where(allowed, scores[head], NEG_FILL))
        weights.append(probs.astype(BF16))
        grad_dot = jnp.sum(weights[head].astype(F32) * prob_grads[head], 0, keepdims=True)
        score_grads.append((probs * (prob_grads[head] - grad_dot)).astype(BF16))
    values = [dot(weights[head], grads[head], NN) for head in heads]
    keys = [dot(score_grads[head], q_ref[:, lanes(head)], NN) * SCALING for head in heads]
    for wide, own_ref, half in (
        (keys, ks_ref, 0),
        (values, vs_ref, 1),
    ):
        for head in heads:
            at = lanes(head)
            own_ref[:, at] = wide[head][rim : rim + queries]
            to_low_ref[half, :, at] = wide[head][:rim].astype(BF16)
            to_high_ref[half, :, at] = wide[head][rim + queries :].astype(BF16)
    for head in heads:
        key = window_of(k_ref, low_ref, high_ref, 0, head)
        query_sum = dot(score_grads[head], key, TN) * SCALING
        qs_ref[:, :, lanes(head)] = chunked(query_sum, qs_ref.shape[0]).astype(BF16)


def same_position(rows, spots):
    left = lax.broadcasted_iota(jnp.int32, (rows, rows), 0)
    right = lax.broadcasted_iota(jnp.int32, (rows, rows), 1)
    return left % spots == right % spots


def temporal_scores_kernel(moved_ref, begun_ref, sent_ref, probs_ref, sem):
    frames, spots = moved_ref.shape[0], moved_ref.shape[1]
    channels = HEADS * HEAD_DIM
    load = started(begun_ref, sent_ref.at[:, :, :channels], sem)
    same = same_position(frames * spots, spots)
    for group in range(HEADS // TIME_HEADS):
        heads = range(group * TIME_HEADS, (group + 1) * TIME_HEADS)
        scores = [
            dot(head_rows(moved_ref, HEADS + head), head_rows(moved_ref, head), NT) for head in heads
        ]
        probs = [softmax_columns(jnp.where(same, part, NEG_FILL)) for part in scores]
        grads = [
            dot(part.astype(BF16), head_rows(moved_ref, 2 * HEADS + head), NN)
            for part, head in zip(probs, heads)
        ]
        for part, head in zip(probs, heads):
            probs_ref[head] = part
        for part, head in zip(grads, heads):
            sent_ref[:, :, lanes(HEADS + head)] = chunked(part, frames).astype(BF16)
    load.wait()


def temporal_grads_kernel(moved_ref, both_ref, probs_ref, out_ref, grad_ref, held, sems):
    frames = moved_ref.shape[0]
    width = TIME_HEADS * HEAD_DIM
    groups = range(HEADS // TIME_HEADS)
    stores = [started(both_ref.at[:, :, HEADS * HEAD_DIM :], grad_ref, sems.at[3 * len(groups)])]
    for group in groups:
        heads = range(group * TIME_HEADS, (group + 1) * TIME_HEADS)
        spatial = [head_rows(both_ref, head) for head in heads]
        prob_grads = [
            dot(part, head_rows(moved_ref, 2 * HEADS + head), NT) for part, head in zip(spatial, heads)
        ]
        outs = [dot(probs_ref[head].astype(BF16), part, TN) for part, head in zip(spatial, heads)]
        score_grads = []
        for prob_grad, head in zip(prob_grads, heads):
            probs = probs_ref[head]
            weights = probs.astype(BF16).astype(F32)
            grad_dot = jnp.sum(weights * prob_grad, 0, keepdims=True)
            score_grads.append((probs * (prob_grad - grad_dot)).astype(BF16))
        query_parts = [
            dot(part, head_rows(moved_ref, HEADS + head), TN) * SCALING
            for part, head in zip(score_grads, heads)
        ]
        key_parts = [
            dot(part, head_rows(moved_ref, head), NN) * SCALING for part, head in zip(score_grads, heads)
        ]
        for place, parts in enumerate((outs, query_parts, key_parts)):
            piece = group * 3 + place
            for step, part in enumerate(parts):
                first = piece * width + step * HEAD_DIM
                held[:, :, first : first + HEAD_DIM] = chunked(part, frames).astype(BF16)
            at = slice(piece * width, (piece + 1) * width)
            stores.append(started(held.at[:, :, at], out_ref.at[:, :, at], sems.at[piece]))
    for store in stores:
        store.wait()


def rims_kernel(k_first_ref, v_first_ref, k_last_ref, v_last_ref, to_low_ref, to_high_ref):
    to_low_ref[0] = k_first_ref[...]
    to_low_ref[1] = v_first_ref[...]
    to_high_ref[0] = k_last_ref[...]
    to_high_ref[1] = v_last_ref[...]


def started(source, target, sem):
    copy = pltpu.make_async_copy(source, target, sem)
    copy.start()
    return copy


def join_kernel(*refs):
    sources, (joined_ref, held, load_sems, store_sems) = refs[:-4], refs[-4:]
    pieces = load_sems.shape[0]
    chunks, width = joined_ref.shape[0] // pieces, sources[0].shape[2]
    loads = []
    for piece in range(pieces):
        rows = slice(piece * chunks, (piece + 1) * chunks)
        loads.append(
            [
                started(
                    source.at[rows],
                    held.at[rows, :, place * width : (place + 1) * width],
                    load_sems.at[piece, place],
                )
                for place, source in enumerate(sources)
            ]
        )
    stores = []
    for piece in range(pieces):
        rows = slice(piece * chunks, (piece + 1) * chunks)
        for load in loads[piece]:
            load.wait()
        stores.append(started(held.at[rows], joined_ref.at[rows], store_sems.at[piece]))
    for store in stores:
        store.wait()


def rim_add_kernel(ks_ref, vs_ref, from_low_ref, from_high_ref, key_ref, value_ref):
    rim = from_low_ref.shape[1]
    rows = ks_ref.shape[0]
    totals = [
        jnp.concatenate(
            [
                sum_ref[:rim] + from_low_ref[half].astype(F32),
                sum_ref[rim : rows - rim],
                sum_ref[rows - rim :] + from_high_ref[half].astype(F32),
            ],
            0,
        )
        for half, sum_ref in enumerate((ks_ref, vs_ref))
    ]
    key_ref[...] = chunked(totals[0], key_ref.shape[0]).astype(BF16)
    value_ref[...] = totals[1].astype(BF16)


def last_sum_kernel(back_ref, qs_ref, ks_ref, *refs):
    outs, (back, qs, ks), results, (load_sems, store_sems) = refs[:3], refs[3:6], refs[6:8], refs[8:]
    pieces = load_sems.shape[0]
    chunks = back.shape[0] // pieces
    width = TIME_HEADS * HEAD_DIM
    groups = range(HEADS // TIME_HEADS)
    pairs = ((back_ref, back), (qs_ref, qs), (ks_ref, ks))
    somes = [slice(piece * chunks, (piece + 1) * chunks) for piece in range(pieces)]
    loads, stores = [], []
    for piece, some in enumerate(somes):
        loads.append(
            [
                started(source.at[some], target.at[some], load_sems.at[piece, place])
                for place, (source, target) in enumerate(pairs)
            ]
        )
    for piece, some in enumerate(somes):
        for load in loads[piece]:
            load.wait()
        for group in groups:
            to = slice(group * width, (group + 1) * width)
            first = group * 3 * width
            stores.append(
                started(
                    back.at[some, :, first : first + width],
                    outs[0].at[some, :, to],
                    store_sems.at[piece, group],
                )
            )
            for place, (kept, result) in enumerate(((qs, results[0]), (ks, results[1]))):
                first += width
                part = back[some, :, first : first + width].astype(F32)
                result[some, :, to] = (part + kept[some, :, to].astype(F32)).astype(BF16)
        for place in range(2):
            stores.append(
                started(
                    results[place].at[some],
                    outs[1 + place].at[some],
                    store_sems.at[piece, len(groups) + place],
                )
            )
    for store in stores:
        store.wait()


def in_hbm(tensor):
    return pltpu.with_memory_space_constraint(tensor, pltpu.HBM)


def in_vmem(tensor):
    return pltpu.with_memory_space_constraint(tensor, pltpu.VMEM)


def exchange(chunks):
    return lax.all_to_all(chunks, "tm", split_axis=0, concat_axis=0, tiled=True)


def on_device(queries, key_states, value_states, out_grad):
    band_rows, breadth, channels = queries.shape[1:]
    tokens = band_rows * breadth
    rim = RADIUS * breadth
    parts = lax.axis_size("tm")
    bands = lax.axis_size("rows")
    spots = tokens // parts
    band = lax.axis_index("rows").astype(jnp.int32)
    first_row = (band * band_rows).reshape(1)
    total_rows = bands * band_rows
    upward = [(i, i + 1) for i in range(bands - 1)]
    downward = [(i + 1, i) for i in range(bands - 1)]

    scalar = pl.BlockSpec(memory_space=pltpu.SMEM)
    anywhere = pl.BlockSpec(memory_space=pl.ANY)

    def rows_block(rows, heads):
        return pl.BlockSpec((rows, heads * HEAD_DIM), lambda i: (0, i))

    def rims_block(heads):
        return pl.BlockSpec((2, rim, heads * HEAD_DIM), lambda i: (0, 0, i))

    def chunk_block(heads, offset, stride=1):
        return pl.BlockSpec((parts, spots, heads * HEAD_DIM), lambda i: (0, 0, i * stride + offset))

    query, key, value = (
        tensor.reshape(tokens, channels) for tensor in (queries, key_states, value_states)
    )
    rims = jax.ShapeDtypeStruct((2, rim, channels), BF16)
    first_rows = pl.BlockSpec((breadth, channels), lambda i: (i, 0))
    last_rows = pl.BlockSpec((breadth, channels), lambda i: (i + band_rows - RADIUS, 0))
    rim_rows = pl.BlockSpec((2, breadth, channels), lambda i: (0, i, 0))
    to_low, to_high = call(
        rims_kernel,
        RADIUS,
        [first_rows, first_rows, last_rows, last_rows],
        [rim_rows, rim_rows],
        [pltpu.HBM(rims.shape, BF16)] * 2,
    )(*map(in_hbm, (key, value, key, value)))
    low = lax.ppermute(to_high, "rows", upward)
    high = lax.ppermute(to_low, "rows", downward)

    joined_shape = (parts, spots, 3 * channels)
    joined = pl.pallas_call(
        join_kernel,
        in_specs=[anywhere] * 3,
        out_specs=anywhere,
        out_shape=pltpu.HBM(joined_shape, BF16),
        scratch_shapes=[
            pltpu.VMEM(joined_shape, BF16),
            pltpu.SemaphoreType.DMA((PIECES, 3)),
            pltpu.SemaphoreType.DMA((PIECES,)),
        ],
        compiler_params=params,
    )(*(in_hbm(tensor.reshape(parts, spots, channels)) for tensor in (queries, key_states, out_grad)))
    moved = exchange(joined)

    own = rows_block(tokens, FWD_HEADS)
    spatial = call(
        functools.partial(spatial_fwd_kernel, total_rows, breadth),
        HEADS // FWD_HEADS,
        [scalar, own, own, own, rims_block(FWD_HEADS), rims_block(FWD_HEADS)],
        chunk_block(FWD_HEADS, 0),
        pltpu.HBM((parts, spots, channels), BF16),
    )(first_row, query, key, value, low, high)

    moved = in_vmem(moved)
    groups = HEADS // TIME_HEADS
    in_place = pl.BlockSpec(memory_space=pltpu.VMEM)
    sent, probs = pl.pallas_call(
        temporal_scores_kernel,
        in_specs=[in_place, anywhere],
        out_specs=[in_place, in_place],
        out_shape=[
            pltpu.VMEM((parts, spots, 2 * channels), BF16),
            pltpu.VMEM((HEADS, tokens, tokens), F32),
        ],
        scratch_shapes=[pltpu.SemaphoreType.DMA],
        compiler_params=params,
    )(moved, in_hbm(spatial))
    both = in_vmem(exchange(sent))

    parts_out, spatial_grad = pl.pallas_call(
        temporal_grads_kernel,
        in_specs=[in_place] * 3,
        out_specs=[anywhere] * 2,
        out_shape=[pltpu.HBM(joined_shape, BF16), pltpu.HBM((parts, spots, channels), BF16)],
        scratch_shapes=[pltpu.VMEM(joined_shape, BF16), pltpu.SemaphoreType.DMA((3 * groups + 1,))],
        compiler_params=params,
    )(moved, both, in_vmem(probs))
    back = exchange(parts_out)

    count = HEADS // BWD_HEADS
    own = rows_block(tokens, BWD_HEADS)
    whole = jax.ShapeDtypeStruct((tokens, channels), F32)
    qs, ks, vs, to_low, to_high = call(
        functools.partial(spatial_bwd_kernel, total_rows, breadth),
        count,
        [scalar, own, own, own, rims_block(BWD_HEADS), rims_block(BWD_HEADS), chunk_block(BWD_HEADS, 0)],
        [chunk_block(BWD_HEADS, 0), own, own, rims_block(BWD_HEADS), rims_block(BWD_HEADS)],
        [pltpu.HBM((parts, spots, channels), BF16), whole, whole, rims, rims],
    )(first_row, query, key, value, low, high, in_hbm(spatial_grad))
    from_high = lax.ppermute(to_low, "rows", downward)
    from_low = lax.ppermute(to_high, "rows", upward)
    final = jax.ShapeDtypeStruct((tokens, channels), BF16)
    own = rows_block(tokens, RIM_HEADS)
    ks, value_grad = call(
        rim_add_kernel,
        HEADS // RIM_HEADS,
        [own, own, rims_block(RIM_HEADS), rims_block(RIM_HEADS)],
        [chunk_block(RIM_HEADS, 0), own],
        [pltpu.HBM((parts, spots, channels), BF16), final],
    )(ks, vs, from_low, from_high)

    temporal_out, query_grad, key_grad = pl.pallas_call(
        last_sum_kernel,
        in_specs=[anywhere] * 3,
        out_specs=[anywhere] * 3,
        out_shape=[pltpu.HBM((parts, spots, channels), BF16)] * 3,
        scratch_shapes=[pltpu.VMEM(joined_shape, BF16)]
        + [pltpu.VMEM((parts, spots, channels), BF16)] * 4
        + [pltpu.SemaphoreType.DMA((PIECES, 3)), pltpu.SemaphoreType.DMA((PIECES, groups + 2))],
        compiler_params=params,
    )(back, in_hbm(qs), in_hbm(ks))
    return tuple(
        tensor.reshape(queries.shape) for tensor in (temporal_out, query_grad, key_grad, value_grad)
    )


def solution(mesh):
    placed = P("tm", "rows", None, None)
    return jax.shard_map(
        on_device,
        mesh=mesh,
        in_specs=(placed,) * 4,
        out_specs=(placed,) * 4,
        check_vma=False,
    )
```
